32 devices in a mesh: table: 4 (over y, x), replica: 8 (over z, core).
Axes of the slice: x: 2, y: 2, z: 4, core: 2. Of those that a mesh axis runs over, the one named last changes fastest.
Arguments:
- embeds: bfloat16 [2048, 512], P('replica', 'table'), may hold values from -6 to 6
- cotangent: bfloat16 [2048, 512], P('replica', 'table'), may hold values from -6 to 6
- send_plan: int32 [8, 4, 8], P('replica'), may hold values from 0 to 7, each once within a row
- work_plan: int32 [8, 4, 8], P('replica', 'table'), may hold values from 0 to 7, each once within a row
- sequence_tiles: int32 [8, 4, 4], P('replica', 'table'), may hold values from 1 to 4, 8 in all within a row
- slopes: float32 [8], replicated, may hold values from 0.002 to 0.2
- uvqk_weight: bfloat16 [512, 2048], replicated, may hold values from -0.25 to 0.25
- out_weight: bfloat16 [512, 512], replicated, may hold values from -0.25 to 0.25
Outputs:
- layer_output: bfloat16 [2048, 512], P('replica', 'table')
- input_gradient: bfloat16 [2048, 512], P('replica', 'table')
The draws below stay inside these ranges and needn't reach their ends.
Inputs may be any that keep to these rules, and one draw needn't show every extreme that they name: `send_plan`: a device's 8 entries are all different. `work_plan`: a device's 8 entries are all different. `sequence_tiles`: a device's 4 entries sum to 8.
All inputs are finite; a program needn't handle non-finite values.
Results may differ from the reference program's by a relative error of at most 0.013.
Values may be sent and summed in bfloat16 or wider, within the bound.
A program may use at most 64 MiB of HBM per device.

```python
import math
import jax
import jax.numpy as jnp
import numpy as np
from jax import lax

D = 512
HEADS = 8
TILE = 8
PEER_TILES = 1
SEQ_DEV = 4
TILES_DEV = 8
TOK_DEV = 64
REPLICAS = 8
TABLES = 4
TOKENS = 2048
N_TABLE = 4
N_REPLICA = 8


def level_of(own_key, extent, cuts, least, high):
    gain = 1.0
    for dim, blocks in cuts:
        draws = jax.random.uniform(jax.random.fold_in(jax.random.fold_in(own_key, 6), dim), (blocks,), jnp.float32, least / len(cuts), high / len(cuts))
        gain = gain * jnp.repeat(jnp.exp(draws), extent[dim] // blocks).reshape((-1,) + (1,) * (len(extent) - 1 - dim))
    return gain


def length_profile(amount, total, bound, slope):
    portions = [(1 << 20) // math.isqrt(standing ** slope) + 1 for standing in range(2, amount + 1)]
    rest, holding = total - bound - (amount - 1), [1] * (amount - 1)
    while rest > 0:
        movable = [i for i in range(amount - 1) if holding[i] < bound]
        mass, remaining = sum([portions[i] for i in movable]), rest
        for i in movable:
            more = min(bound - holding[i], max(1, remaining * portions[i] // mass), rest)
            holding[i] = holding[i] + more
            rest = rest - more
    return np.array([bound] + holding)


def ragged_sizes(key, amount, total, limit, slope):
    if amount == 2:
        one = jax.random.randint(key, (), max(1, total - limit), min(limit, total - 1) + 1)
        return jnp.stack([one, total - one])
    tallies = jnp.asarray(length_profile(amount, total, limit, slope), jnp.int32)
    couples = (amount - 1) // 2
    donor, receiver = tallies[1:1 + 2 * couples:2], tallies[2:2 + 2 * couples:2]
    slack = jnp.minimum(donor - 1, limit - receiver)
    passed = jax.random.randint(jax.random.fold_in(key, 1), (couples,), 0, 1 << 20) % (slack + 1)
    tallies = tallies.at[1:1 + 2 * couples:2].set(donor - passed).at[2:2 + 2 * couples:2].set(receiver + passed)
    return tallies[jax.random.permutation(jax.random.fold_in(key, 2), amount)]


def noise(own_key, dims, width, bound, split=(), held_as=jnp.bfloat16):
    factor_of = level_of(own_key, dims, split, -0.22, 0.18) if split else 1.0
    array = jax.random.normal(own_key, dims, jnp.float32) * width * factor_of
    return jnp.minimum(jnp.maximum(array, -bound), bound).astype(held_as)


def setup_inputs(seed: int = 0) -> dict:
    splits = jax.random.split(jax.random.key(seed), 9)
    return {
        "embeds": noise(splits[0], (TOKENS, D), 1.0, 6.0, ((0, 8), (1, 4))),
        "cotangent": noise(splits[1], (TOKENS, D), 1.0, 6.0, ((0, 8), (1, 4))),
        "send_plan": jax.vmap(lambda own: jax.random.permutation(own, TILES_DEV))(jax.random.split(splits[2], REPLICAS * TABLES)).reshape((REPLICAS, TABLES, TILES_DEV)).astype(jnp.int32),
        "work_plan": jax.vmap(lambda own: jax.random.permutation(own, TILES_DEV))(jax.random.split(splits[3], REPLICAS * TABLES)).reshape((REPLICAS, TABLES, TILES_DEV)).astype(jnp.int32),
        "sequence_tiles": jax.vmap(lambda own: ragged_sizes(own, SEQ_DEV, TILES_DEV, TILES_DEV // 2, 2))(jax.random.split(splits[4], REPLICAS * TABLES)).reshape((REPLICAS, TABLES, SEQ_DEV)).astype(jnp.int32),
        "slopes": jnp.clip(jnp.exp(jax.random.uniform(splits[5], (HEADS,), jnp.float32, math.log(0.002), math.log(0.2))), 0.002, 0.2),
        "uvqk_weight": noise(splits[6], (D, 4 * D), D ** -0.5, 0.25),
        "out_weight": noise(splits[7], (D, D), D ** -0.5, 0.25),
    }


EPSILON = 1e-05

def layer_norm(features):
    centre = lax.optimization_barrier(jnp.mean(features, axis=-1, keepdims=True))
    centred = features - centre
    spread = lax.optimization_barrier(jnp.mean(centred * centred, axis=-1, keepdims=True))
    return centred * lax.rsqrt(spread + EPSILON)

def segment_ids(lengths, row_count, tile_rows):
    boundary = jnp.cumsum(lengths.astype(jnp.int32))
    tile_index = jnp.arange(row_count, dtype=jnp.int32) // tile_rows
    return lax.optimization_barrier(jnp.sum((tile_index[None, :] >= boundary[:, None]).astype(jnp.int32), axis=0))

def hstu_layer(inputs, segment, slopes, uvqk_weight, out_weight):
    row_count, feature_count = inputs.shape
    head_count = slopes.shape[0]
    head_size = feature_count // head_count
    score_scale = head_size ** (-0.5)
    normed = layer_norm(inputs.astype(jnp.float32)).astype(jnp.bfloat16)
    projected = jax.nn.silu(jnp.dot(normed, uvqk_weight, preferred_element_type=jnp.float32))
    gate_part = projected[:, :feature_count]
    value_part = projected[:, feature_count:2 * feature_count].astype(jnp.bfloat16)
    query_part = projected[:, 2 * feature_count:3 * feature_count].astype(jnp.bfloat16)
    key_part = projected[:, 3 * feature_count:].astype(jnp.bfloat16)
    row_index = lax.broadcasted_iota(jnp.int32, (row_count, row_count), 0)
    col_index = lax.broadcasted_iota(jnp.int32, (row_count, row_count), 1)
    allowed = (segment[:, None] == segment[None, :]) & (col_index <= row_index)
    distance = (row_index - col_index).astype(jnp.float32)
    pieces = []
    for head_index in range(head_count):
        lower = head_index * head_size
        upper = lower + head_size
        scores = jnp.dot(query_part[:, lower:upper], key_part[:, lower:upper].T, preferred_element_type=jnp.float32)
        scores = scores * score_scale - slopes[head_index] * distance
        weights = jnp.where(allowed, jax.nn.silu(scores), jnp.zeros_like(scores)).astype(jnp.bfloat16)
        pieces.append(jnp.dot(weights, value_part[:, lower:upper], preferred_element_type=jnp.float32))
    attended = jnp.concatenate(pieces, axis=1)
    gated = (layer_norm(attended) * gate_part).astype(jnp.bfloat16)
    mixing = jnp.dot(gated, out_weight, preferred_element_type=jnp.float32)
    return (inputs.astype(jnp.float32) + mixing).astype(jnp.bfloat16)

def forward_backward(inputs, grad_rows, segment, slopes, uvqk_weight, out_weight):

    def apply_layer(layer_input):
        return hstu_layer(layer_input, segment, slopes, uvqk_weight, out_weight)
    outputs, pullback = jax.vjp(apply_layer, inputs)
    return (outputs, pullback(grad_rows)[0])

def reference(embeds, cotangent, send_plan, work_plan, sequence_tiles, slopes, uvqk_weight, out_weight):
    table_count = N_TABLE
    replica_count = N_REPLICA
    device_count = replica_count * table_count
    dest_index = jnp.arange(replica_count, dtype=jnp.int32)[:, None, None]
    table_index = jnp.arange(table_count, dtype=jnp.int32)[None, :, None]
    source_index = (work_plan // PEER_TILES).astype(jnp.int32)
    place_index = (work_plan % PEER_TILES).astype(jnp.int32)
    home_tile = send_plan[source_index, table_index, dest_index * PEER_TILES + place_index].astype(jnp.int32)
    flat_index = ((source_index * table_count + table_index) * TILES_DEV + home_tile).reshape(-1).astype(jnp.int32)
    home_inputs = embeds.reshape(-1, TILE, D)
    home_grads = cotangent.reshape(-1, TILE, D)
    work_inputs = home_inputs[flat_index].reshape(device_count, TOK_DEV, D)
    work_grads = home_grads[flat_index].reshape(device_count, TOK_DEV, D)
    lengths = sequence_tiles.reshape(device_count, SEQ_DEV)

    def one_device(packed):
        inputs, grad_rows, counts = packed
        segment = segment_ids(counts, TOK_DEV, TILE)
        return forward_backward(inputs, grad_rows, segment, slopes, uvqk_weight, out_weight)
    outputs, gradient = lax.map(one_device, (work_inputs, work_grads, lengths))
    layer_output = jnp.zeros_like(home_inputs).at[flat_index].set(outputs.reshape(-1, TILE, D)).reshape(embeds.shape)
    input_gradient = jnp.zeros_like(home_grads).at[flat_index].set(gradient.reshape(-1, TILE, D)).reshape(embeds.shape)
    return (layer_output, input_gradient)
```

```python
import functools

import jax
import jax.numpy as jnp
from jax import lax
from jax.experimental import pallas as pl
from jax.experimental.pallas import tpu as pltpu
from jax.sharding import PartitionSpec as P

MESH = pl.DeviceIdType.MESH
MXU = 256
LANES = 128
F32 = jnp.float32
BF16 = jnp.bfloat16

TILE = 8


EPSILON = 1e-05


def layer_norm(features):
    centre = jnp.mean(features, axis=-1, keepdims=True)
    centred = features - centre
    spread = jnp.mean(centred * centred, axis=-1, keepdims=True)
    return centred * lax.rsqrt(spread + EPSILON)


def segment_ids(lengths, row_count, tile_rows):
    boundary = jnp.cumsum(lengths)
    tile_index = jnp.arange(row_count, dtype=jnp.int32) // tile_rows
    return jnp.sum((tile_index[None, :] >= boundary[:, None]).astype(jnp.int32), axis=0)


def hstu_layer(inputs, segment, slopes, uvqk_weight, out_weight):
    row_count, feature_count = inputs.shape
    head_count = slopes.shape[0]
    head_size = feature_count // head_count
    score_scale = head_size ** (-0.5)
    normed = layer_norm(inputs.astype(jnp.float32)).astype(jnp.bfloat16)
    projected = jax.nn.silu(jnp.dot(normed, uvqk_weight, preferred_element_type=jnp.float32))
    gate_part = projected[:, :feature_count]
    value_part = projected[:, feature_count : 2 * feature_count].astype(jnp.bfloat16)
    query_part = projected[:, 2 * feature_count : 3 * feature_count].astype(jnp.bfloat16)
    key_part = projected[:, 3 * feature_count :].astype(jnp.bfloat16)
    row_index = lax.broadcasted_iota(jnp.int32, (row_count, row_count), 0)
    col_index = lax.broadcasted_iota(jnp.int32, (row_count, row_count), 1)
    allowed = (segment[:, None] == segment[None, :]) & (col_index <= row_index)
    distance = (row_index - col_index).astype(jnp.float32)
    pieces = []
    for head_index in range(head_count):
        lower = head_index * head_size
        upper = lower + head_size
        scores = jnp.dot(
            query_part[:, lower:upper],
            key_part[:, lower:upper].T,
            preferred_element_type=jnp.float32,
        )
        scores = scores * score_scale - slopes[head_index] * distance
        weights = jnp.where(allowed, jax.nn.silu(scores), jnp.zeros_like(scores)).astype(
            jnp.bfloat16
        )
        pieces.append(
            jnp.dot(weights, value_part[:, lower:upper], preferred_element_type=jnp.float32)
        )
    attended = jnp.concatenate(pieces, axis=1)
    gated = (layer_norm(attended) * gate_part).astype(jnp.bfloat16)
    mixing = jnp.dot(gated, out_weight, preferred_element_type=jnp.float32)
    return (inputs.astype(jnp.float32) + mixing).astype(jnp.bfloat16)


def forward_backward(inputs, grad_rows, segment, slopes, uvqk_weight, out_weight):

    def apply_layer(layer_input):
        return hstu_layer(layer_input, segment, slopes, uvqk_weight, out_weight)

    outputs, pullback = jax.vjp(apply_layer, inputs)
    return (outputs, pullback(grad_rows)[0])


def shards(
    embeds, cotangent, send_plan, work_plan, sequence_tiles, slopes, uvqk_weight, out_weight
):
    table_count = lax.axis_size("table")
    replica_count = lax.axis_size("replica")
    column_count = embeds.shape[1]
    row_count = embeds.shape[0] // table_count
    tile_count = row_count // TILE
    peer_rows = row_count // replica_count
    feature_count = column_count * table_count
    block_plans = send_plan[0]
    own_send = lax.dynamic_index_in_dim(block_plans, lax.axis_index("table"), 0, keepdims=False)
    own_work = work_plan[0, 0]
    segment = segment_ids(sequence_tiles[0, 0], row_count, TILE)
    tile_order = jnp.arange(tile_count, dtype=jnp.int32)
    row_inputs, row_grads = (
        lax.all_to_all(embeds, "table", split_axis=0, concat_axis=1, tiled=True),
        lax.all_to_all(cotangent, "table", split_axis=0, concat_axis=1, tiled=True),
    )

    def to_slots(shard_rows):
        tiled = shard_rows.reshape(tile_count, TILE, feature_count)
        return tiled[own_send]

    got_inputs, got_grads = (
        lax.all_to_all(to_slots(row_inputs), "replica", split_axis=0, concat_axis=0, tiled=True),
        lax.all_to_all(to_slots(row_grads), "replica", split_axis=0, concat_axis=0, tiled=True),
    )
    work_inputs = got_inputs[own_work].reshape(row_count, feature_count)
    work_grads = got_grads[own_work].reshape(row_count, feature_count)
    outputs, gradient = forward_backward(
        work_inputs, work_grads, segment, slopes, uvqk_weight, out_weight
    )
    undo_work = jnp.zeros((tile_count,), jnp.int32).at[own_work].set(tile_order)

    def to_sources(result):
        return result.reshape(tile_count, TILE, feature_count)[undo_work]

    slot_outputs = to_sources(outputs)
    slot_grads = to_sources(gradient)
    back_outputs, back_grads = (
        lax.all_to_all(slot_outputs, "replica", split_axis=0, concat_axis=0, tiled=True),
        lax.all_to_all(slot_grads, "replica", split_axis=0, concat_axis=0, tiled=True),
    )
    undo_send = jnp.zeros((tile_count,), jnp.int32).at[own_send].set(tile_order)

    def to_home(result):
        return result[undo_send].reshape(row_count, feature_count)

    layer_output, input_gradient = (
        lax.all_to_all(to_home(back_outputs), "table", split_axis=1, concat_axis=0, tiled=True),
        lax.all_to_all(to_home(back_grads), "table", split_axis=1, concat_axis=0, tiled=True),
    )
    return (layer_output, input_gradient)


NT = (((1,), (1,)), ((), ()))
TN = (((0,), (0,)), ((), ()))


def mm(a, b, dims=(((1,), (0,)), ((), ()))):
    return lax.dot_general(a, b, dims, preferred_element_type=F32)


def norm_parts(features):
    centred = features - jnp.mean(features, axis=-1, keepdims=True)
    scale = lax.rsqrt(jnp.mean(centred * centred, axis=-1, keepdims=True) + EPSILON)
    return centred * scale, scale


def norm_back(grad, normal, scale):
    along = jnp.mean(grad * normal, axis=-1, keepdims=True)
    return scale * (grad - jnp.mean(grad, axis=-1, keepdims=True) - normal * along)


def silu_parts(v):
    sig = 0.5 * jnp.tanh(0.5 * v) + 0.5
    value = v * sig
    return value, sig + value * (1.0 - sig)


def fused_kernel(
    T, R, H,
    send_ref, work_ref, seq_ref, slope_ref, emb_ref, cot_ref, wu_hbm, wo_hbm,
    out_ref, grad_ref,
    wu, wo, emb32, cot32, stage, got, x_s, dy_s, slope_s, back, ret, inv,
    w_sem, send_sem, recv_sem, send_sem2, recv_sem2,
):
    n = T * R
    rows = R * TILE
    width = emb_ref.shape[1]
    feat = T * width
    hs = feat // H
    G = max(1, min(H, MXU // max(hs, rows)))
    gw, gr = G * hs, G * rows
    scale = hs ** (-0.5)
    me_t = lax.axis_index("table")
    me_r = lax.axis_index("replica")
    me = me_r * T + me_t

    wu_copy = pltpu.make_async_copy(wu_hbm, wu, w_sem.at[0])
    wo_copy = pltpu.make_async_copy(wo_hbm, wo, w_sem.at[1])
    wu_copy.start()
    wo_copy.start()

    def peer(off):
        other = lax.rem(me + off, n)
        return other, {"table": lax.rem(other, T), "replica": other // T}

    barrier = pltpu.get_barrier_semaphore()

    def greet(off, carry):
        pl.semaphore_signal(barrier, inc=1, device_id=peer(off)[1], device_id_type=MESH)
        return carry

    lax.fori_loop(1, n, greet, 0)

    emb32[...] = emb_ref[...].astype(F32).reshape(emb32.shape)
    cot32[...] = cot_ref[...].astype(F32).reshape(cot32.shape)
    for d in range(R):
        for t in range(T):
            k = t * R + send_ref[0, t, d]
            stage[d * T + t] = jnp.concatenate([emb32[k], cot32[k]], axis=0).astype(BF16)

    pl.semaphore_wait(barrier, n - 1)

    def post(src, dst, s_sem, r_sem):
        def one(off, carry):
            other, device = peer(off)
            pltpu.make_async_remote_copy(
                src_ref=src.at[other],
                dst_ref=dst.at[me],
                send_sem=s_sem,
                recv_sem=r_sem,
                device_id=device,
                device_id_type=MESH,
            ).start()
            return carry

        lax.fori_loop(1, n, one, 0)
        dst[me] = src[me]

    def settle(ref, sem):
        part = ref.at[pl.ds(0, n - 1)]
        pltpu.make_async_copy(part, part, sem).wait()

    post(stage, got, send_sem, recv_sem)

    for t in range(T):
        for j in range(R):
            found = jnp.int32(0)
            for d in range(1, R):
                found = jnp.where(send_ref[0, t, d] == j, d, found)
            inv[t, j] = found

    bounds = []
    total = jnp.int32(0)
    for j in range(seq_ref.shape[2]):
        total = total + seq_ref[0, 0, j]
        bounds.append(total)

    def places(index):
        slot = index // TILE
        place = jnp.zeros_like(index)
        for w in range(1, R):
            place = jnp.where(slot == work_ref[0, 0, w], w, place)
        segment = jnp.zeros_like(index)
        for bound in bounds:
            segment = segment + (place >= bound).astype(jnp.int32)
        return place * TILE + index % TILE, segment

    row_pos, row_seg = places(lax.broadcasted_iota(jnp.int32, (rows, 1), 0))
    lane = lax.broadcasted_iota(jnp.int32, (1, gr), 1)
    col_pos, col_seg = places(lane % rows)
    distance = (row_pos - col_pos).astype(F32)
    allowed = (row_seg == col_seg) & (col_pos <= row_pos)
    slope_s[...] = jnp.where(allowed, distance, -1.0)
    same_head = (
        lax.broadcasted_iota(jnp.int32, (gr, gw), 0) // rows
        == lax.broadcasted_iota(jnp.int32, (gr, gw), 1) // hs
    )
    head_mask = jnp.where(same_head, 1.0, 0.0)
    head_mask16 = head_mask.astype(BF16)

    def spread(block):
        return jnp.concatenate([block] * G, axis=0) * head_mask16

    def collect(full):
        masked = full * head_mask
        total = masked[:rows]
        for h in range(1, G):
            total = total + masked[h * rows : (h + 1) * rows]
        return total

    settle(got, recv_sem)
    for s in range(R):
        for t in range(T):
            piece = got[s * T + t].astype(F32)
            rs, cs = slice(s * TILE, (s + 1) * TILE), slice(t * width, (t + 1) * width)
            x_s[rs, cs] = piece[:TILE]
            dy_s[rs, cs] = piece[TILE:]

    x = x_s[...]
    normal, x_scale = norm_parts(x)
    normed = normal.astype(BF16)
    wu_copy.wait()
    wo_copy.wait()
    projected, slopes_back = [], []
    for c in range(4):
        block = mm(normed, wu[:, c * feat : (c + 1) * feat])
        value, deriv = silu_parts(block)
        projected.append(value if c == 0 else value.astype(BF16))
        slopes_back.append(deriv)
    gate, value, query, key = projected

    relative = slope_s[...]
    allowed = relative >= 0.0
    weights, derivs, pieces, values, keys, queries = [], [], [], [], [], []
    for g in range(H // G):
        cs = slice(g * gw, (g + 1) * gw)
        kd, vd, q = spread(key[:, cs]), spread(value[:, cs]), query[:, cs]
        slope = jnp.zeros((1, gr), F32)
        for h in range(G):
            slope = jnp.where(lane // rows == h, slope_ref[g * G + h], slope)
        scores = mm(q, kd, NT) * scale - slope * relative
        weight, deriv = silu_parts(scores)
        weight = jnp.where(allowed, weight, 0.0).astype(BF16)
        derivs.append(jnp.where(allowed, deriv * scale, 0.0))
        weights.append(weight)
        pieces.append(mm(weight, vd))
        keys.append(kd)
        values.append(vd)
        queries.append(q)
    attended, att_scale = norm_parts(jnp.concatenate(pieces, axis=1))
    gated = (attended * gate).astype(BF16)
    output = x + mm(gated, wo[...])

    dy = dy_s[...]
    dgated = mm(dy.astype(BF16), wo[...], NT).astype(BF16).astype(F32)
    dgate = dgated * attended
    datt = norm_back(dgated * gate, attended, att_scale).astype(BF16)
    dv, dq, dk = [], [], []
    for g in range(H // G):
        da = datt[:, g * gw : (g + 1) * gw]
        dw = mm(da, values[g], NT).astype(BF16).astype(F32)
        ds = (dw * derivs[g]).astype(BF16)
        dv.append(collect(mm(weights[g], da, TN)))
        dq.append(mm(ds, keys[g]))
        dk.append(collect(mm(ds, queries[g], TN)))
    dprojected = [dgate] + [
        jnp.concatenate(parts, axis=1).astype(BF16).astype(F32) for parts in (dv, dq, dk)
    ]
    dnormed = jnp.zeros_like(x)
    for c in range(4):
        dz = (dprojected[c] * slopes_back[c]).astype(BF16)
        dnormed = dnormed + mm(dz, wu[:, c * feat : (c + 1) * feat], NT)
    dnormed = dnormed.astype(BF16).astype(F32)
    gradient = norm_back(dnormed, normal, x_scale) + dy

    for s in range(R):
        for t in range(T):
            rs, cs = slice(s * TILE, (s + 1) * TILE), slice(t * width, (t + 1) * width)
            back[s * T + t] = jnp.concatenate([output[rs, cs], gradient[rs, cs]], axis=0).astype(BF16)
    post(back, ret, send_sem2, recv_sem2)
    settle(ret, recv_sem2)
    for t in range(T):
        for j in range(0, R, 2):
            first = ret[inv[t, j] * T + t].astype(F32)
            second = ret[inv[t, j + 1] * T + t].astype(F32)
            at = slice(t * rows + j * TILE, t * rows + (j + 2) * TILE)
            out_ref[at, :] = jnp.concatenate([first[:TILE], second[:TILE]], axis=0).astype(BF16)
            grad_ref[at, :] = jnp.concatenate([first[TILE:], second[TILE:]], axis=0).astype(BF16)
    settle(stage, send_sem)
    settle(back, send_sem2)


def fused_shards(
    embeds, cotangent, send_plan, work_plan, sequence_tiles, slopes, uvqk_weight, out_weight
):
    T, R = lax.axis_size("table"), lax.axis_size("replica")
    n, rows, width = T * R, R * TILE, embeds.shape[1]
    feat, H = T * width, slopes.shape[0]
    G = max(1, min(H, MXU // max(feat // H, rows)))
    vmem = pl.BlockSpec(memory_space=pltpu.VMEM)
    smem = pl.BlockSpec(memory_space=pltpu.SMEM)
    hbm = pl.BlockSpec(memory_space=pl.ANY)
    message = pltpu.VMEM((n, 2 * TILE, width), BF16)
    return pl.pallas_call(
        functools.partial(fused_kernel, T, R, H),
        out_shape=(
            jax.ShapeDtypeStruct(embeds.shape, BF16),
            jax.ShapeDtypeStruct(embeds.shape, BF16),
        ),
        in_specs=[smem, smem, smem, smem, vmem, vmem, hbm, hbm],
        out_specs=(vmem, vmem),
        scratch_shapes=[
            pltpu.VMEM(uvqk_weight.shape, BF16),
            pltpu.VMEM(out_weight.shape, BF16),
            pltpu.VMEM((n, TILE, width), F32),
            pltpu.VMEM((n, TILE, width), F32),
            message,
            message,
            pltpu.VMEM((rows, feat), F32),
            pltpu.VMEM((rows, feat), F32),
            pltpu.VMEM((rows, G * rows), F32),
            message,
            message,
            pltpu.SMEM((T, R), jnp.int32),
            pltpu.SemaphoreType.DMA((2,)),
            pltpu.SemaphoreType.DMA,
            pltpu.SemaphoreType.DMA,
            pltpu.SemaphoreType.DMA,
            pltpu.SemaphoreType.DMA,
        ],
        compiler_params=pltpu.CompilerParams(
            collective_id=0, has_side_effects=True, vmem_limit_bytes=48 << 20
        ),
        name="hstu_fused",
    )(send_plan, work_plan, sequence_tiles, slopes, embeds, cotangent, uvqk_weight, out_weight)


def fits_fused(embeds, slopes, T, R):
    width = embeds.shape[1]
    heads = slopes.shape[0]
    row_count = embeds.shape[0] // T
    head_size = width * T // heads
    return (
        width % LANES == 0
        and R % 2 == 0
        and row_count == R * TILE
        and head_size == row_count
        and heads % max(1, min(heads, MXU // head_size)) == 0
    )


def routed(embeds, cotangent, send_plan, work_plan, sequence_tiles, slopes, *weights):
    T, R = lax.axis_size("table"), lax.axis_size("replica")
    body = fused_shards if fits_fused(embeds, slopes, T, R) else shards
    return body(embeds, cotangent, send_plan, work_plan, sequence_tiles, slopes, *weights)


def solution(mesh):
    in_specs = (
        P("replica", "table"),
        P("replica", "table"),
        P("replica", None, None),
        P("replica", "table", None),
        P("replica", "table", None),
        P(),
        P(),
        P(),
    )
    out_specs = (P("replica", "table"), P("replica", "table"))
    return jax.shard_map(routed, mesh=mesh, in_specs=in_specs, out_specs=out_specs, check_vma=False)
```

```python
import functools

import jax
import jax.numpy as jnp
from jax import lax
from jax.experimental import pallas as pl
from jax.experimental.pallas import tpu as pltpu
from jax.sharding import PartitionSpec as P

MESH = pl.DeviceIdType.MESH
MXU = 256
LANES = 128
VMEM_BYTES = 64 << 20
F32 = jnp.float32
BF16 = jnp.bfloat16

TILE = 8


EPSILON = 1e-05


def layer_norm(features):
    centre = jnp.mean(features, axis=-1, keepdims=True)
    centred = features - centre
    spread = jnp.mean(centred * centred, axis=-1, keepdims=True)
    return centred * lax.rsqrt(spread + EPSILON)


def segment_ids(lengths, row_count, tile_rows):
    boundary = jnp.cumsum(lengths)
    tile_index = jnp.arange(row_count, dtype=jnp.int32) // tile_rows
    return jnp.sum((tile_index[None, :] >= boundary[:, None]).astype(jnp.int32), axis=0)


def hstu_layer(inputs, segment, slopes, uvqk_weight, out_weight):
    row_count, feature_count = inputs.shape
    head_count = slopes.shape[0]
    head_size = feature_count // head_count
    score_scale = head_size ** (-0.5)
    normed = layer_norm(inputs.astype(jnp.float32)).astype(jnp.bfloat16)
    projected = jax.nn.silu(jnp.dot(normed, uvqk_weight, preferred_element_type=jnp.float32))
    gate_part = projected[:, :feature_count]
    value_part = projected[:, feature_count : 2 * feature_count].astype(jnp.bfloat16)
    query_part = projected[:, 2 * feature_count : 3 * feature_count].astype(jnp.bfloat16)
    key_part = projected[:, 3 * feature_count :].astype(jnp.bfloat16)
    row_index = lax.broadcasted_iota(jnp.int32, (row_count, row_count), 0)
    col_index = lax.broadcasted_iota(jnp.int32, (row_count, row_count), 1)
    allowed = (segment[:, None] == segment[None, :]) & (col_index <= row_index)
    distance = (row_index - col_index).astype(jnp.float32)
    pieces = []
    for head_index in range(head_count):
        lower = head_index * head_size
        upper = lower + head_size
        scores = jnp.dot(
            query_part[:, lower:upper],
            key_part[:, lower:upper].T,
            preferred_element_type=jnp.float32,
        )
        scores = scores * score_scale - slopes[head_index] * distance
        weights = jnp.where(allowed, jax.nn.silu(scores), jnp.zeros_like(scores)).astype(
            jnp.bfloat16
        )
        pieces.append(
            jnp.dot(weights, value_part[:, lower:upper], preferred_element_type=jnp.float32)
        )
    attended = jnp.concatenate(pieces, axis=1)
    gated = (layer_norm(attended) * gate_part).astype(jnp.bfloat16)
    mixing = jnp.dot(gated, out_weight, preferred_element_type=jnp.float32)
    return (inputs.astype(jnp.float32) + mixing).astype(jnp.bfloat16)


def forward_backward(inputs, grad_rows, segment, slopes, uvqk_weight, out_weight):

    def apply_layer(layer_input):
        return hstu_layer(layer_input, segment, slopes, uvqk_weight, out_weight)

    outputs, pullback = jax.vjp(apply_layer, inputs)
    return (outputs, pullback(grad_rows)[0])


def shards(
    embeds, cotangent, send_plan, work_plan, sequence_tiles, slopes, uvqk_weight, out_weight
):
    table_count = lax.axis_size("table")
    replica_count = lax.axis_size("replica")
    column_count = embeds.shape[1]
    row_count = embeds.shape[0] // table_count
    tile_count = row_count // TILE
    peer_rows = row_count // replica_count
    feature_count = column_count * table_count
    block_plans = send_plan[0]
    own_send = lax.dynamic_index_in_dim(block_plans, lax.axis_index("table"), 0, keepdims=False)
    own_work = work_plan[0, 0]
    segment = segment_ids(sequence_tiles[0, 0], row_count, TILE)
    tile_order = jnp.arange(tile_count, dtype=jnp.int32)
    row_inputs, row_grads = (
        lax.all_to_all(embeds, "table", split_axis=0, concat_axis=1, tiled=True),
        lax.all_to_all(cotangent, "table", split_axis=0, concat_axis=1, tiled=True),
    )

    def to_slots(shard_rows):
        tiled = shard_rows.reshape(tile_count, TILE, feature_count)
        return tiled[own_send]

    got_inputs, got_grads = (
        lax.all_to_all(to_slots(row_inputs), "replica", split_axis=0, concat_axis=0, tiled=True),
        lax.all_to_all(to_slots(row_grads), "replica", split_axis=0, concat_axis=0, tiled=True),
    )
    work_inputs = got_inputs[own_work].reshape(row_count, feature_count)
    work_grads = got_grads[own_work].reshape(row_count, feature_count)
    outputs, gradient = forward_backward(
        work_inputs, work_grads, segment, slopes, uvqk_weight, out_weight
    )
    undo_work = jnp.zeros((tile_count,), jnp.int32).at[own_work].set(tile_order)

    def to_sources(result):
        return result.reshape(tile_count, TILE, feature_count)[undo_work]

    slot_outputs = to_sources(outputs)
    slot_grads = to_sources(gradient)
    back_outputs, back_grads = (
        lax.all_to_all(slot_outputs, "replica", split_axis=0, concat_axis=0, tiled=True),
        lax.all_to_all(slot_grads, "replica", split_axis=0, concat_axis=0, tiled=True),
    )
    undo_send = jnp.zeros((tile_count,), jnp.int32).at[own_send].set(tile_order)

    def to_home(result):
        return result[undo_send].reshape(row_count, feature_count)

    layer_output, input_gradient = (
        lax.all_to_all(to_home(back_outputs), "table", split_axis=1, concat_axis=0, tiled=True),
        lax.all_to_all(to_home(back_grads), "table", split_axis=1, concat_axis=0, tiled=True),
    )
    return (layer_output, input_gradient)


NT = (((1,), (1,)), ((), ()))
TN = (((0,), (0,)), ((), ()))


def mm(a, b, dims=(((1,), (0,)), ((), ()))):
    return lax.dot_general(a, b, dims, preferred_element_type=F32)


def norm_parts(features):
    centred = features - jnp.mean(features, axis=-1, keepdims=True)
    scale = lax.rsqrt(jnp.mean(centred * centred, axis=-1, keepdims=True) + EPSILON)
    return centred * scale, scale


def norm_back(grad, normal, scale):
    along = jnp.mean(grad * normal, axis=-1, keepdims=True)
    return scale * (grad - jnp.mean(grad, axis=-1, keepdims=True) - normal * along)


def silu_parts(v):
    sig = 0.5 * jnp.tanh(0.5 * v) + 0.5
    value = v * sig
    return value, sig + value * (1.0 - sig)


def fused_kernel(
    T, R, H,
    send_hbm, work_hbm, seq_hbm, slope_hbm, emb_hbm, cot_hbm, wu_hbm, wo_hbm,
    ret,
    send_ref, work_ref, seq_ref, slope_ref, emb_ref, cot_ref,
    wu, wo, emb32, cot32, stage, got, x_s, dy_s, slope_s, back,
    in_sem, own_sem, send_sem, recv_sem, send_sem2, recv_sem2,
):
    n = T * R
    rows = R * TILE
    width = emb_ref.shape[1]
    feat = T * width
    hs = feat // H
    G = max(1, min(H, MXU // max(hs, rows)))
    gw, gr = G * hs, G * rows
    scale = hs ** (-0.5)
    me_t = lax.axis_index("table")
    me_r = lax.axis_index("replica")
    me = me_r * T + me_t

    sources = (send_hbm, emb_hbm, cot_hbm, work_hbm, seq_hbm, slope_hbm, wu_hbm, wo_hbm)
    targets = (send_ref, emb_ref, cot_ref, work_ref, seq_ref, slope_ref, wu, wo)
    loads = [
        pltpu.make_async_copy(source, target, in_sem.at[i])
        for i, (source, target) in enumerate(zip(sources, targets))
    ]
    for load in loads:
        load.start()

    peers = []
    for far in range(R - 1, -1, -1):
        for near in range(T):
            if far or near:
                t, r = lax.rem(me_t + near, T), lax.rem(me_r + far, R)
                peers.append((r * T + t, {"table": t, "replica": r}))

    barrier = pltpu.get_barrier_semaphore()
    for _, device in peers:
        pl.semaphore_signal(barrier, inc=1, device_id=device, device_id_type=MESH)

    for load in loads[:3]:
        load.wait()

    emb32[...] = emb_ref[...].astype(F32).reshape(emb32.shape)
    cot32[...] = cot_ref[...].astype(F32).reshape(cot32.shape)
    for d in range(R):
        for t in range(T):
            k = t * R + send_ref[0, t, d]
            stage[d * T + t] = jnp.concatenate([emb32[k], cot32[k]], axis=0).astype(BF16)

    pl.semaphore_wait(barrier, n - 1)

    def post(src, dst, s_sem, r_sem):
        for other, device in peers:
            pltpu.make_async_remote_copy(
                src_ref=src.at[other],
                dst_ref=dst.at[me],
                send_sem=s_sem,
                recv_sem=r_sem,
                device_id=device,
                device_id_type=MESH,
            ).start()

    def settle(ref, sem):
        part = ref.at[pl.ds(0, n - 1)]
        pltpu.make_async_copy(part, part, sem).wait()

    post(stage, got, send_sem, recv_sem)
    got[me] = stage[me]

    for load in loads[3:6]:
        load.wait()
    bounds = []
    total = jnp.int32(0)
    for j in range(seq_ref.shape[2]):
        total = total + seq_ref[0, 0, j]
        bounds.append(total)

    def places(index):
        slot = index // TILE
        place = jnp.zeros_like(index)
        for w in range(1, R):
            place = jnp.where(slot == work_ref[0, 0, w], w, place)
        segment = jnp.zeros_like(index)
        for bound in bounds:
            segment = segment + (place >= bound).astype(jnp.int32)
        return place * TILE + index % TILE, segment

    row_pos, row_seg = places(lax.broadcasted_iota(jnp.int32, (rows, 1), 0))
    lane = lax.broadcasted_iota(jnp.int32, (1, gr), 1)
    col_pos, col_seg = places(lane % rows)
    distance = (row_pos - col_pos).astype(F32)
    allowed = (row_seg == col_seg) & (col_pos <= row_pos)
    slope_s[...] = jnp.where(allowed, distance, -1.0)
    same_head = (
        lax.broadcasted_iota(jnp.int32, (gr, gw), 0) // rows
        == lax.broadcasted_iota(jnp.int32, (gr, gw), 1) // hs
    )
    head_mask = jnp.where(same_head, 1.0, 0.0)
    head_mask16 = head_mask.astype(BF16)

    def spread(block):
        return jnp.concatenate([block] * G, axis=0) * head_mask16

    def collect(full):
        masked = full * head_mask
        total = masked[:rows]
        for h in range(1, G):
            total = total + masked[h * rows : (h + 1) * rows]
        return total

    settle(got, recv_sem)
    for s in range(R):
        for t in range(T):
            piece = got[s * T + t].astype(F32)
            rs, cs = slice(s * TILE, (s + 1) * TILE), slice(t * width, (t + 1) * width)
            x_s[rs, cs] = piece[:TILE]
            dy_s[rs, cs] = piece[TILE:]

    x = x_s[...]
    normal, x_scale = norm_parts(x)
    normed = normal.astype(BF16)
    for load in loads[6:]:
        load.wait()
    projected, slopes_back = [], []
    for c in range(4):
        block = mm(normed, wu[:, c * feat : (c + 1) * feat])
        value, deriv = silu_parts(block)
        projected.append(value if c == 0 else value.astype(BF16))
        slopes_back.append(deriv)
    gate, value, query, key = projected

    relative = slope_s[...]
    allowed = relative >= 0.0
    weights, derivs, pieces, values, keys, queries = [], [], [], [], [], []
    for g in range(H // G):
        cs = slice(g * gw, (g + 1) * gw)
        kd, vd, q = spread(key[:, cs]), spread(value[:, cs]), query[:, cs]
        slope = jnp.zeros((1, gr), F32)
        for h in range(G):
            slope = jnp.where(lane // rows == h, slope_ref[g * G + h], slope)
        scores = mm(q, kd, NT) * scale - slope * relative
        weight, deriv = silu_parts(scores)
        weight = jnp.where(allowed, weight, 0.0).astype(BF16)
        derivs.append(jnp.where(allowed, deriv * scale, 0.0))
        weights.append(weight)
        pieces.append(mm(weight, vd))
        keys.append(kd)
        values.append(vd)
        queries.append(q)
    attended, att_scale = norm_parts(jnp.concatenate(pieces, axis=1))
    gated = (attended * gate).astype(BF16)
    output = x + mm(gated, wo[...])

    dy = dy_s[...]
    dgated = mm(dy.astype(BF16), wo[...], NT).astype(BF16).astype(F32)
    dgate = dgated * attended
    datt = norm_back(dgated * gate, attended, att_scale).astype(BF16)
    dv, dq, dk = [], [], []
    for g in range(H // G):
        da = datt[:, g * gw : (g + 1) * gw]
        dw = mm(da, values[g], NT).astype(BF16).astype(F32)
        ds = (dw * derivs[g]).astype(BF16)
        dv.append(collect(mm(weights[g], da, TN)))
        dq.append(mm(ds, keys[g]))
        dk.append(collect(mm(ds, queries[g], TN)))
    dprojected = [dgate] + [
        jnp.concatenate(parts, axis=1).astype(BF16).astype(F32) for parts in (dv, dq, dk)
    ]
    dnormed = jnp.zeros_like(x)
    for c in range(4):
        dz = (dprojected[c] * slopes_back[c]).astype(BF16)
        dnormed = dnormed + mm(dz, wu[:, c * feat : (c + 1) * feat], NT)
    dnormed = dnormed.astype(BF16).astype(F32)
    gradient = norm_back(dnormed, normal, x_scale) + dy

    for s in range(R):
        for t in range(T):
            rs, cs = slice(s * TILE, (s + 1) * TILE), slice(t * width, (t + 1) * width)
            back[s * T + t] = jnp.concatenate([output[rs, cs], gradient[rs, cs]], axis=0).astype(BF16)
    post(back, ret, send_sem2, recv_sem2)
    own = pltpu.make_async_copy(back.at[me], ret.at[me], own_sem)
    own.start()
    own.wait()
    settle(ret, recv_sem2)
    settle(stage, send_sem)
    settle(back, send_sem2)


def fused_shards(
    embeds, cotangent, send_plan, work_plan, sequence_tiles, slopes, uvqk_weight, out_weight
):
    T, R = lax.axis_size("table"), lax.axis_size("replica")
    n, rows, width = T * R, R * TILE, embeds.shape[1]
    feat, H = T * width, slopes.shape[0]
    G = max(1, min(H, MXU // max(feat // H, rows)))
    vmem = pl.BlockSpec(memory_space=pltpu.VMEM)
    smem = pl.BlockSpec(memory_space=pltpu.SMEM)
    hbm = pl.BlockSpec(memory_space=pltpu.HBM)
    message = pltpu.VMEM((n, 2 * TILE, width), BF16)
    ret = pl.pallas_call(
        functools.partial(fused_kernel, T, R, H),
        out_shape=jax.ShapeDtypeStruct((n, 2 * TILE, width), BF16),
        in_specs=[hbm] * 8,
        out_specs=hbm,
        scratch_shapes=[
            pltpu.SMEM(send_plan.shape, jnp.int32),
            pltpu.SMEM(work_plan.shape, jnp.int32),
            pltpu.SMEM(sequence_tiles.shape, jnp.int32),
            pltpu.SMEM(slopes.shape, F32),
            pltpu.VMEM(embeds.shape, BF16),
            pltpu.VMEM(cotangent.shape, BF16),
            pltpu.VMEM(uvqk_weight.shape, BF16),
            pltpu.VMEM(out_weight.shape, BF16),
            pltpu.VMEM((n, TILE, width), F32),
            pltpu.VMEM((n, TILE, width), F32),
            message,
            message,
            pltpu.VMEM((rows, feat), F32),
            pltpu.VMEM((rows, feat), F32),
            pltpu.VMEM((rows, G * rows), F32),
            message,
            pltpu.SemaphoreType.DMA((8,)),
            pltpu.SemaphoreType.DMA,
            pltpu.SemaphoreType.DMA,
            pltpu.SemaphoreType.DMA,
            pltpu.SemaphoreType.DMA,
            pltpu.SemaphoreType.DMA,
        ],
        compiler_params=pltpu.CompilerParams(
            collective_id=0, has_side_effects=True, vmem_limit_bytes=VMEM_BYTES
        ),
        name="hstu_fused",
    )(send_plan, work_plan, sequence_tiles, slopes, embeds, cotangent, uvqk_weight, out_weight)
    return pl.pallas_call(
        functools.partial(place_kernel, T, R),
        out_shape=(
            jax.ShapeDtypeStruct(embeds.shape, BF16),
            jax.ShapeDtypeStruct(embeds.shape, BF16),
        ),
        in_specs=[smem, vmem],
        out_specs=(vmem, vmem),
        scratch_shapes=[
            pltpu.VMEM((n, TILE, width), F32),
            pltpu.VMEM((n, TILE, width), F32),
        ],
        compiler_params=pltpu.CompilerParams(vmem_limit_bytes=VMEM_BYTES),
        name="place",
    )(send_plan, ret)


def place_kernel(T, R, send_ref, ret_ref, out_ref, grad_ref, out32, grad32):
    for t in range(T):
        for d in range(R):
            piece = ret_ref[d * T + t].astype(F32)
            k = t * R + send_ref[0, t, d]
            out32[k] = piece[:TILE]
            grad32[k] = piece[TILE:]
    out_ref[...] = out32[...].reshape(out_ref.shape).astype(BF16)
    grad_ref[...] = grad32[...].reshape(grad_ref.shape).astype(BF16)


def fits_fused(embeds, slopes, T, R):
    width = embeds.shape[1]
    heads = slopes.shape[0]
    row_count = embeds.shape[0] // T
    head_size = width * T // heads
    return (
        width % LANES == 0
        and R % 2 == 0
        and row_count == R * TILE
        and head_size == row_count
        and heads % max(1, min(heads, MXU // head_size)) == 0
    )


def routed(embeds, cotangent, send_plan, work_plan, sequence_tiles, slopes, *weights):
    T, R = lax.axis_size("table"), lax.axis_size("replica")
    body = fused_shards if fits_fused(embeds, slopes, T, R) else shards
    return body(embeds, cotangent, send_plan, work_plan, sequence_tiles, slopes, *weights)


def solution(mesh):
    in_specs = (
        P("replica", "table"),
        P("replica", "table"),
        P("replica", None, None),
        P("replica", "table", None),
        P("replica", "table", None),
        P(),
        P(),
        P(),
    )
    out_specs = (P("replica", "table"), P("replica", "table"))
    return jax.shard_map(routed, mesh=mesh, in_specs=in_specs, out_specs=out_specs, check_vma=False)
```

```python
import functools

import jax
import jax.numpy as jnp
from jax import lax
from jax.experimental import pallas as pl
from jax.experimental.pallas import tpu as pltpu
from jax.sharding import PartitionSpec as P

MESH = pl.DeviceIdType.MESH
MXU = 256
LANES = 128
VMEM_BYTES = 64 << 20
F32 = jnp.float32
BF16 = jnp.bfloat16

TILE = 8


EPSILON = 1e-05


def layer_norm(features):
    centre = jnp.mean(features, axis=-1, keepdims=True)
    centred = features - centre
    spread = jnp.mean(centred * centred, axis=-1, keepdims=True)
    return centred * lax.rsqrt(spread + EPSILON)


def segment_ids(lengths, row_count, tile_rows):
    boundary = jnp.cumsum(lengths)
    tile_index = jnp.arange(row_count, dtype=jnp.int32) // tile_rows
    return jnp.sum((tile_index[None, :] >= boundary[:, None]).astype(jnp.int32), axis=0)


def hstu_layer(inputs, segment, slopes, uvqk_weight, out_weight):
    row_count, feature_count = inputs.shape
    head_count = slopes.shape[0]
    head_size = feature_count // head_count
    score_scale = head_size ** (-0.5)
    normed = layer_norm(inputs.astype(jnp.float32)).astype(jnp.bfloat16)
    projected = jax.nn.silu(jnp.dot(normed, uvqk_weight, preferred_element_type=jnp.float32))
    gate_part = projected[:, :feature_count]
    value_part = projected[:, feature_count : 2 * feature_count].astype(jnp.bfloat16)
    query_part = projected[:, 2 * feature_count : 3 * feature_count].astype(jnp.bfloat16)
    key_part = projected[:, 3 * feature_count :].astype(jnp.bfloat16)
    row_index = lax.broadcasted_iota(jnp.int32, (row_count, row_count), 0)
    col_index = lax.broadcasted_iota(jnp.int32, (row_count, row_count), 1)
    allowed = (segment[:, None] == segment[None, :]) & (col_index <= row_index)
    distance = (row_index - col_index).astype(jnp.float32)
    pieces = []
    for head_index in range(head_count):
        lower = head_index * head_size
        upper = lower + head_size
        scores = jnp.dot(
            query_part[:, lower:upper],
            key_part[:, lower:upper].T,
            preferred_element_type=jnp.float32,
        )
        scores = scores * score_scale - slopes[head_index] * distance
        weights = jnp.where(allowed, jax.nn.silu(scores), jnp.zeros_like(scores)).astype(
            jnp.bfloat16
        )
        pieces.append(
            jnp.dot(weights, value_part[:, lower:upper], preferred_element_type=jnp.float32)
        )
    attended = jnp.concatenate(pieces, axis=1)
    gated = (layer_norm(attended) * gate_part).astype(jnp.bfloat16)
    mixing = jnp.dot(gated, out_weight, preferred_element_type=jnp.float32)
    return (inputs.astype(jnp.float32) + mixing).astype(jnp.bfloat16)


def forward_backward(inputs, grad_rows, segment, slopes, uvqk_weight, out_weight):

    def apply_layer(layer_input):
        return hstu_layer(layer_input, segment, slopes, uvqk_weight, out_weight)

    outputs, pullback = jax.vjp(apply_layer, inputs)
    return (outputs, pullback(grad_rows)[0])


def shards(
    embeds, cotangent, send_plan, work_plan, sequence_tiles, slopes, uvqk_weight, out_weight
):
    table_count = lax.axis_size("table")
    replica_count = lax.axis_size("replica")
    column_count = embeds.shape[1]
    row_count = embeds.shape[0] // table_count
    tile_count = row_count // TILE
    peer_rows = row_count // replica_count
    feature_count = column_count * table_count
    block_plans = send_plan[0]
    own_send = lax.dynamic_index_in_dim(block_plans, lax.axis_index("table"), 0, keepdims=False)
    own_work = work_plan[0, 0]
    segment = segment_ids(sequence_tiles[0, 0], row_count, TILE)
    tile_order = jnp.arange(tile_count, dtype=jnp.int32)
    row_inputs, row_grads = (
        lax.all_to_all(embeds, "table", split_axis=0, concat_axis=1, tiled=True),
        lax.all_to_all(cotangent, "table", split_axis=0, concat_axis=1, tiled=True),
    )

    def to_slots(shard_rows):
        tiled = shard_rows.reshape(tile_count, TILE, feature_count)
        return tiled[own_send]

    got_inputs, got_grads = (
        lax.all_to_all(to_slots(row_inputs), "replica", split_axis=0, concat_axis=0, tiled=True),
        lax.all_to_all(to_slots(row_grads), "replica", split_axis=0, concat_axis=0, tiled=True),
    )
    work_inputs = got_inputs[own_work].reshape(row_count, feature_count)
    work_grads = got_grads[own_work].reshape(row_count, feature_count)
    outputs, gradient = forward_backward(
        work_inputs, work_grads, segment, slopes, uvqk_weight, out_weight
    )
    undo_work = jnp.zeros((tile_count,), jnp.int32).at[own_work].set(tile_order)

    def to_sources(result):
        return result.reshape(tile_count, TILE, feature_count)[undo_work]

    slot_outputs = to_sources(outputs)
    slot_grads = to_sources(gradient)
    back_outputs, back_grads = (
        lax.all_to_all(slot_outputs, "replica", split_axis=0, concat_axis=0, tiled=True),
        lax.all_to_all(slot_grads, "replica", split_axis=0, concat_axis=0, tiled=True),
    )
    undo_send = jnp.zeros((tile_count,), jnp.int32).at[own_send].set(tile_order)

    def to_home(result):
        return result[undo_send].reshape(row_count, feature_count)

    layer_output, input_gradient = (
        lax.all_to_all(to_home(back_outputs), "table", split_axis=1, concat_axis=0, tiled=True),
        lax.all_to_all(to_home(back_grads), "table", split_axis=1, concat_axis=0, tiled=True),
    )
    return (layer_output, input_gradient)


NT = (((1,), (1,)), ((), ()))
TN = (((0,), (0,)), ((), ()))


def mm(a, b, dims=(((1,), (0,)), ((), ()))):
    return lax.dot_general(a, b, dims, preferred_element_type=F32)


def norm_parts(features):
    centred = features - jnp.mean(features, axis=-1, keepdims=True)
    scale = lax.rsqrt(jnp.mean(centred * centred, axis=-1, keepdims=True) + EPSILON)
    return centred * scale, scale


def norm_back(grad, normal, scale):
    along = jnp.mean(grad * normal, axis=-1, keepdims=True)
    return scale * (grad - jnp.mean(grad, axis=-1, keepdims=True) - normal * along)


def silu_parts(v):
    sig = 0.5 * jnp.tanh(0.5 * v) + 0.5
    value = v * sig
    return value, sig + value * (1.0 - sig)


def fused_kernel(
    T, R, H,
    send_hbm, work_hbm, seq_hbm, slope_hbm, emb_hbm, cot_hbm, wu_hbm, wo_hbm,
    out_ret, grad_ret,
    send_ref, work_ref, seq_ref, slope_ref, emb_ref, cot_ref,
    wu, wo, emb32, cot32, emb_stage, cot_stage, emb_got, cot_got, x_s, dy_s, slope_s,
    out_back, grad_back,
    in_sem, own_sem, send_sem, recv_sem,
):
    n = T * R
    rows = R * TILE
    width = emb_ref.shape[1]
    feat = T * width
    hs = feat // H
    G = max(1, min(H, MXU // max(hs, rows)))
    gw, gr = G * hs, G * rows
    scale = hs ** (-0.5)
    me_t = lax.axis_index("table")
    me_r = lax.axis_index("replica")
    me = me_r * T + me_t

    sources = (send_hbm, emb_hbm, cot_hbm, work_hbm, seq_hbm, slope_hbm, wu_hbm, wo_hbm)
    targets = (send_ref, emb_ref, cot_ref, work_ref, seq_ref, slope_ref, wu, wo)
    loads = [
        pltpu.make_async_copy(source, target, in_sem.at[i])
        for i, (source, target) in enumerate(zip(sources, targets))
    ]
    for load in loads[:6]:
        load.start()

    peers = []
    for far in range(R - 1, -1, -1):
        for near in range(T):
            if far or near:
                t, r = lax.rem(me_t + near, T), lax.rem(me_r + far, R)
                peers.append((r * T + t, {"table": t, "replica": r}))

    barrier = pltpu.get_barrier_semaphore()
    for _, device in peers:
        pl.semaphore_signal(barrier, inc=1, device_id=device, device_id_type=MESH)

    def gather(source, source32, target):
        source32[...] = source[...].astype(F32).reshape(source32.shape)
        for d in range(R):
            for t in range(T):
                target[d * T + t] = source32[t * R + send_ref[0, t, d]].astype(BF16)

    loads[0].wait()
    loads[1].wait()
    gather(emb_ref, emb32, emb_stage)
    pl.semaphore_wait(barrier, n - 1)

    def post(src, dst, index):
        for other, device in peers:
            pltpu.make_async_remote_copy(
                src_ref=src.at[other],
                dst_ref=dst.at[me],
                send_sem=send_sem.at[index],
                recv_sem=recv_sem.at[index],
                device_id=device,
                device_id_type=MESH,
            ).start()

    def settle(ref, sem):
        part = ref.at[pl.ds(0, n - 1)]
        pltpu.make_async_copy(part, part, sem).wait()

    def scatter(source, target):
        for s in range(R):
            for t in range(T):
                target[s * T + t] = source[
                    s * TILE : (s + 1) * TILE, t * width : (t + 1) * width
                ].astype(BF16)

    def unpack(source, target):
        for s in range(R):
            for t in range(T):
                target[s * TILE : (s + 1) * TILE, t * width : (t + 1) * width] = source[
                    s * T + t
                ].astype(F32)

    post(emb_stage, emb_got, 0)
    emb_got[me] = emb_stage[me]
    loads[2].wait()
    gather(cot_ref, cot32, cot_stage)
    post(cot_stage, cot_got, 1)
    cot_got[me] = cot_stage[me]
    for load in loads[6:]:
        load.start()

    for load in loads[3:6]:
        load.wait()
    bounds = []
    total = jnp.int32(0)
    for j in range(seq_ref.shape[2]):
        total = total + seq_ref[0, 0, j]
        bounds.append(total)

    def places(index):
        slot = index // TILE
        place = jnp.zeros_like(index)
        for w in range(1, R):
            place = jnp.where(slot == work_ref[0, 0, w], w, place)
        segment = jnp.zeros_like(index)
        for bound in bounds:
            segment = segment + (place >= bound).astype(jnp.int32)
        return place * TILE + index % TILE, segment

    row_pos, row_seg = places(lax.broadcasted_iota(jnp.int32, (rows, 1), 0))
    lane = lax.broadcasted_iota(jnp.int32, (1, gr), 1)
    col_pos, col_seg = places(lane % rows)
    distance = (row_pos - col_pos).astype(F32)
    allowed = (row_seg == col_seg) & (col_pos <= row_pos)
    slope_s[...] = jnp.where(allowed, distance, -1.0)
    same_head = (
        lax.broadcasted_iota(jnp.int32, (gr, gw), 0) // rows
        == lax.broadcasted_iota(jnp.int32, (gr, gw), 1) // hs
    )
    head_mask = jnp.where(same_head, 1.0, 0.0)
    head_mask16 = head_mask.astype(BF16)

    def spread(block):
        return jnp.concatenate([block] * G, axis=0) * head_mask16

    def collect(full):
        masked = full * head_mask
        total = masked[:rows]
        for h in range(1, G):
            total = total + masked[h * rows : (h + 1) * rows]
        return total

    settle(emb_got, recv_sem.at[0])
    unpack(emb_got, x_s)
    x = x_s[...]
    normal, x_scale = norm_parts(x)
    normed = normal.astype(BF16)
    for load in loads[6:]:
        load.wait()
    projected, slopes_back = [], []
    for c in range(4):
        block = mm(normed, wu[:, c * feat : (c + 1) * feat])
        value, deriv = silu_parts(block)
        projected.append(value if c == 0 else value.astype(BF16))
        slopes_back.append(deriv)
    gate, value, query, key = projected

    relative = slope_s[...]
    allowed = relative >= 0.0
    weights, derivs, pieces, values, keys, queries = [], [], [], [], [], []
    for g in range(H // G):
        cs = slice(g * gw, (g + 1) * gw)
        kd, vd, q = spread(key[:, cs]), spread(value[:, cs]), query[:, cs]
        slope = jnp.zeros((1, gr), F32)
        for h in range(G):
            slope = jnp.where(lane // rows == h, slope_ref[g * G + h], slope)
        scores = mm(q, kd, NT) * scale - slope * relative
        weight, deriv = silu_parts(scores)
        weight = jnp.where(allowed, weight, 0.0).astype(BF16)
        derivs.append(jnp.where(allowed, deriv * scale, 0.0))
        weights.append(weight)
        pieces.append(mm(weight, vd))
        keys.append(kd)
        values.append(vd)
        queries.append(q)
    attended, att_scale = norm_parts(jnp.concatenate(pieces, axis=1))
    gated = (attended * gate).astype(BF16)
    output = x + mm(gated, wo[...])

    scatter(output, out_back)
    post(out_back, out_ret, 2)
    out_own = pltpu.make_async_copy(out_back.at[me], out_ret.at[me], own_sem.at[0])
    out_own.start()

    settle(cot_got, recv_sem.at[1])
    unpack(cot_got, dy_s)
    dy = dy_s[...]
    dgated = mm(dy.astype(BF16), wo[...], NT).astype(BF16).astype(F32)
    dgate = dgated * attended
    datt = norm_back(dgated * gate, attended, att_scale).astype(BF16)
    dv, dq, dk = [], [], []
    for g in range(H // G):
        da = datt[:, g * gw : (g + 1) * gw]
        dw = mm(da, values[g], NT).astype(BF16).astype(F32)
        ds = (dw * derivs[g]).astype(BF16)
        dv.append(collect(mm(weights[g], da, TN)))
        dq.append(mm(ds, keys[g]))
        dk.append(collect(mm(ds, queries[g], TN)))
    dprojected = [dgate] + [
        jnp.concatenate(parts, axis=1).astype(BF16).astype(F32) for parts in (dv, dq, dk)
    ]
    dnormed = jnp.zeros_like(x)
    for c in range(4):
        dz = (dprojected[c] * slopes_back[c]).astype(BF16)
        dnormed = dnormed + mm(dz, wu[:, c * feat : (c + 1) * feat], NT)
    dnormed = dnormed.astype(BF16).astype(F32)
    gradient = norm_back(dnormed, normal, x_scale) + dy

    scatter(gradient, grad_back)
    post(grad_back, grad_ret, 3)
    grad_own = pltpu.make_async_copy(grad_back.at[me], grad_ret.at[me], own_sem.at[1])
    grad_own.start()
    out_own.wait()
    grad_own.wait()
    for index, source in enumerate((emb_stage, cot_stage, out_back, grad_back)):
        settle(source, send_sem.at[index])
    settle(out_ret, recv_sem.at[2])
    settle(grad_ret, recv_sem.at[3])


def fused_shards(
    embeds, cotangent, send_plan, work_plan, sequence_tiles, slopes, uvqk_weight, out_weight
):
    T, R = lax.axis_size("table"), lax.axis_size("replica")
    n, rows, width = T * R, R * TILE, embeds.shape[1]
    feat, H = T * width, slopes.shape[0]
    G = max(1, min(H, MXU // max(feat // H, rows)))
    smem = pl.BlockSpec(memory_space=pltpu.SMEM)
    hbm = pl.BlockSpec(memory_space=pltpu.HBM)
    message = pltpu.VMEM((n, TILE, width), BF16)
    tiles = jax.ShapeDtypeStruct((n, TILE, width), BF16)
    results = pl.pallas_call(
        functools.partial(fused_kernel, T, R, H),
        out_shape=(tiles, tiles),
        in_specs=[hbm] * 8,
        out_specs=(hbm, hbm),
        scratch_shapes=[
            pltpu.SMEM(send_plan.shape, jnp.int32),
            pltpu.SMEM(work_plan.shape, jnp.int32),
            pltpu.SMEM(sequence_tiles.shape, jnp.int32),
            pltpu.SMEM(slopes.shape, F32),
            pltpu.VMEM(embeds.shape, BF16),
            pltpu.VMEM(cotangent.shape, BF16),
            pltpu.VMEM(uvqk_weight.shape, BF16),
            pltpu.VMEM(out_weight.shape, BF16),
            pltpu.VMEM((n, TILE, width), F32),
            pltpu.VMEM((n, TILE, width), F32),
            message,
            message,
            message,
            message,
            pltpu.VMEM((rows, feat), F32),
            pltpu.VMEM((rows, feat), F32),
            pltpu.VMEM((rows, G * rows), F32),
            message,
            message,
            pltpu.SemaphoreType.DMA((8,)),
            pltpu.SemaphoreType.DMA((2,)),
            pltpu.SemaphoreType.DMA((4,)),
            pltpu.SemaphoreType.DMA((4,)),
        ],
        compiler_params=pltpu.CompilerParams(
            collective_id=0, has_side_effects=True, vmem_limit_bytes=VMEM_BYTES
        ),
        name="hstu_fused",
    )(send_plan, work_plan, sequence_tiles, slopes, embeds, cotangent, uvqk_weight, out_weight)
    placed = pl.pallas_call(
        functools.partial(place_kernel, T, R),
        out_shape=(tiles, tiles),
        in_specs=[smem, hbm, hbm],
        out_specs=(hbm, hbm),
        scratch_shapes=[pltpu.SemaphoreType.DMA((2,))],
        compiler_params=pltpu.CompilerParams(vmem_limit_bytes=VMEM_BYTES),
        name="place",
    )(send_plan, *results)
    return tuple(part.reshape(embeds.shape) for part in placed)


def place_kernel(T, R, send_ref, out_ret, grad_ret, out_home, grad_home, sem):
    for t in range(T):
        for d in range(R):
            home = t * R + send_ref[0, t, d]
            slot = d * T + t
            pltpu.make_async_copy(out_ret.at[slot], out_home.at[home], sem.at[0]).start()
            pltpu.make_async_copy(grad_ret.at[slot], grad_home.at[home], sem.at[1]).start()
    pltpu.make_async_copy(out_home, out_home, sem.at[0]).wait()
    pltpu.make_async_copy(grad_home, grad_home, sem.at[1]).wait()


def fits_fused(embeds, slopes, T, R):
    width = embeds.shape[1]
    heads = slopes.shape[0]
    row_count = embeds.shape[0] // T
    head_size = width * T // heads
    return (
        width % LANES == 0
        and R % 2 == 0
        and row_count == R * TILE
        and head_size == row_count
        and heads % max(1, min(heads, MXU // head_size)) == 0
    )


def routed(embeds, cotangent, send_plan, work_plan, sequence_tiles, slopes, *weights):
    T, R = lax.axis_size("table"), lax.axis_size("replica")
    body = fused_shards if fits_fused(embeds, slopes, T, R) else shards
    return body(embeds, cotangent, send_plan, work_plan, sequence_tiles, slopes, *weights)


def solution(mesh):
    in_specs = (
        P("replica", "table"),
        P("replica", "table"),
        P("replica", None, None),
        P("replica", "table", None),
        P("replica", "table", None),
        P(),
        P(),
        P(),
    )
    out_specs = (P("replica", "table"), P("replica", "table"))
    return jax.shard_map(routed, mesh=mesh, in_specs=in_specs, out_specs=out_specs, check_vma=False)
```

```python
import functools

import jax
import jax.numpy as jnp
from jax import lax
from jax.experimental import pallas as pl
from jax.experimental.pallas import tpu as pltpu
from jax.sharding import PartitionSpec as P

MESH = pl.DeviceIdType.MESH
MXU = 256
LANES = 128
VMEM_BYTES = 64 << 20
F32 = jnp.float32
BF16 = jnp.bfloat16

TILE = 8


EPSILON = 1e-05


def layer_norm(features):
    centre = jnp.mean(features, axis=-1, keepdims=True)
    centred = features - centre
    spread = jnp.mean(centred * centred, axis=-1, keepdims=True)
    return centred * lax.rsqrt(spread + EPSILON)


def segment_ids(lengths, row_count, tile_rows):
    boundary = jnp.cumsum(lengths)
    tile_index = jnp.arange(row_count, dtype=jnp.int32) // tile_rows
    return jnp.sum((tile_index[None, :] >= boundary[:, None]).astype(jnp.int32), axis=0)


def hstu_layer(inputs, segment, slopes, uvqk_weight, out_weight):
    row_count, feature_count = inputs.shape
    head_count = slopes.shape[0]
    head_size = feature_count // head_count
    score_scale = head_size ** (-0.5)
    normed = layer_norm(inputs.astype(jnp.float32)).astype(jnp.bfloat16)
    projected = jax.nn.silu(jnp.dot(normed, uvqk_weight, preferred_element_type=jnp.float32))
    gate_part = projected[:, :feature_count]
    value_part = projected[:, feature_count : 2 * feature_count].astype(jnp.bfloat16)
    query_part = projected[:, 2 * feature_count : 3 * feature_count].astype(jnp.bfloat16)
    key_part = projected[:, 3 * feature_count :].astype(jnp.bfloat16)
    row_index = lax.broadcasted_iota(jnp.int32, (row_count, row_count), 0)
    col_index = lax.broadcasted_iota(jnp.int32, (row_count, row_count), 1)
    allowed = (segment[:, None] == segment[None, :]) & (col_index <= row_index)
    distance = (row_index - col_index).astype(jnp.float32)
    pieces = []
    for head_index in range(head_count):
        lower = head_index * head_size
        upper = lower + head_size
        scores = jnp.dot(
            query_part[:, lower:upper],
            key_part[:, lower:upper].T,
            preferred_element_type=jnp.float32,
        )
        scores = scores * score_scale - slopes[head_index] * distance
        weights = jnp.where(allowed, jax.nn.silu(scores), jnp.zeros_like(scores)).astype(
            jnp.bfloat16
        )
        pieces.append(
            jnp.dot(weights, value_part[:, lower:upper], preferred_element_type=jnp.float32)
        )
    attended = jnp.concatenate(pieces, axis=1)
    gated = (layer_norm(attended) * gate_part).astype(jnp.bfloat16)
    mixing = jnp.dot(gated, out_weight, preferred_element_type=jnp.float32)
    return (inputs.astype(jnp.float32) + mixing).astype(jnp.bfloat16)


def forward_backward(inputs, grad_rows, segment, slopes, uvqk_weight, out_weight):

    def apply_layer(layer_input):
        return hstu_layer(layer_input, segment, slopes, uvqk_weight, out_weight)

    outputs, pullback = jax.vjp(apply_layer, inputs)
    return (outputs, pullback(grad_rows)[0])


def shards(
    embeds, cotangent, send_plan, work_plan, sequence_tiles, slopes, uvqk_weight, out_weight
):
    table_count = lax.axis_size("table")
    replica_count = lax.axis_size("replica")
    column_count = embeds.shape[1]
    row_count = embeds.shape[0] // table_count
    tile_count = row_count // TILE
    peer_rows = row_count // replica_count
    feature_count = column_count * table_count
    block_plans = send_plan[0]
    own_send = lax.dynamic_index_in_dim(block_plans, lax.axis_index("table"), 0, keepdims=False)
    own_work = work_plan[0, 0]
    segment = segment_ids(sequence_tiles[0, 0], row_count, TILE)
    tile_order = jnp.arange(tile_count, dtype=jnp.int32)
    row_inputs, row_grads = (
        lax.all_to_all(embeds, "table", split_axis=0, concat_axis=1, tiled=True),
        lax.all_to_all(cotangent, "table", split_axis=0, concat_axis=1, tiled=True),
    )

    def to_slots(shard_rows):
        tiled = shard_rows.reshape(tile_count, TILE, feature_count)
        return tiled[own_send]

    got_inputs, got_grads = (
        lax.all_to_all(to_slots(row_inputs), "replica", split_axis=0, concat_axis=0, tiled=True),
        lax.all_to_all(to_slots(row_grads), "replica", split_axis=0, concat_axis=0, tiled=True),
    )
    work_inputs = got_inputs[own_work].reshape(row_count, feature_count)
    work_grads = got_grads[own_work].reshape(row_count, feature_count)
    outputs, gradient = forward_backward(
        work_inputs, work_grads, segment, slopes, uvqk_weight, out_weight
    )
    undo_work = jnp.zeros((tile_count,), jnp.int32).at[own_work].set(tile_order)

    def to_sources(result):
        return result.reshape(tile_count, TILE, feature_count)[undo_work]

    slot_outputs = to_sources(outputs)
    slot_grads = to_sources(gradient)
    back_outputs, back_grads = (
        lax.all_to_all(slot_outputs, "replica", split_axis=0, concat_axis=0, tiled=True),
        lax.all_to_all(slot_grads, "replica", split_axis=0, concat_axis=0, tiled=True),
    )
    undo_send = jnp.zeros((tile_count,), jnp.int32).at[own_send].set(tile_order)

    def to_home(result):
        return result[undo_send].reshape(row_count, feature_count)

    layer_output, input_gradient = (
        lax.all_to_all(to_home(back_outputs), "table", split_axis=1, concat_axis=0, tiled=True),
        lax.all_to_all(to_home(back_grads), "table", split_axis=1, concat_axis=0, tiled=True),
    )
    return (layer_output, input_gradient)


NT = (((1,), (1,)), ((), ()))
TN = (((0,), (0,)), ((), ()))


def mm(a, b, dims=(((1,), (0,)), ((), ()))):
    return lax.dot_general(a, b, dims, preferred_element_type=F32)


def norm_parts(features):
    centred = features - jnp.mean(features, axis=-1, keepdims=True)
    scale = lax.rsqrt(jnp.mean(centred * centred, axis=-1, keepdims=True) + EPSILON)
    return centred * scale, scale


def norm_back(grad, normal, scale):
    along = jnp.mean(grad * normal, axis=-1, keepdims=True)
    return scale * (grad - jnp.mean(grad, axis=-1, keepdims=True) - normal * along)


def silu_parts(v):
    sig = 0.5 * jnp.tanh(0.5 * v) + 0.5
    value = v * sig
    return value, sig + value * (1.0 - sig)


def fused_kernel(
    T, R, H,
    send_hbm, work_hbm, seq_hbm, slope_hbm, emb_hbm, cot_hbm, wu_hbm, wo_hbm,
    out_ret, grad_ret,
    send_ref, work_ref, seq_ref, slope_ref, emb_ref, cot_ref,
    wu, wo, emb32, cot32, emb_stage, cot_stage, emb_got, cot_got, x_s, dy_s, slope_s,
    out_back, grad_back,
    in_sem, own_sem, send_sem, recv_sem,
):
    n = T * R
    rows = R * TILE
    width = emb_ref.shape[1]
    feat = T * width
    hs = feat // H
    G = max(1, min(H, MXU // max(hs, rows)))
    gw, gr = G * hs, G * rows
    scale = hs ** (-0.5)
    me_t = lax.axis_index("table")
    me_r = lax.axis_index("replica")
    me = me_r * T + me_t

    sources = (send_hbm, emb_hbm, cot_hbm, work_hbm, seq_hbm, slope_hbm, wu_hbm, wo_hbm)
    targets = (send_ref, emb_ref, cot_ref, work_ref, seq_ref, slope_ref, wu, wo)
    loads = [
        pltpu.make_async_copy(source, target, in_sem.at[i])
        for i, (source, target) in enumerate(zip(sources, targets))
    ]
    for load in loads[:6]:
        load.start()

    peers = []
    for far in range(R - 1, -1, -1):
        for near in range(T):
            if far or near:
                t, r = lax.rem(me_t + near, T), lax.rem(me_r + far, R)
                peers.append((r * T + t, {"table": t, "replica": r}))

    barrier = pltpu.get_barrier_semaphore()
    for _, device in peers:
        pl.semaphore_signal(barrier, inc=1, device_id=device, device_id_type=MESH)

    def gather(source, source32, target):
        source32[...] = source[...].astype(F32).reshape(source32.shape)
        for d in range(R):
            for t in range(T):
                target[d * T + t] = source32[t * R + send_ref[0, t, d]].astype(BF16)

    loads[0].wait()
    loads[1].wait()
    gather(emb_ref, emb32, emb_stage)
    pl.semaphore_wait(barrier, n - 1)

    def post(src, dst, index):
        for other, device in peers:
            pltpu.make_async_remote_copy(
                src_ref=src.at[other],
                dst_ref=dst.at[me],
                send_sem=send_sem.at[index],
                recv_sem=recv_sem.at[index],
                device_id=device,
                device_id_type=MESH,
            ).start()

    def settle(ref, sem):
        part = ref.at[pl.ds(0, n - 1)]
        pltpu.make_async_copy(part, part, sem).wait()

    def scatter(source, target):
        for s in range(R):
            for t in range(T):
                target[s * T + t] = source[
                    s * TILE : (s + 1) * TILE, t * width : (t + 1) * width
                ].astype(BF16)

    def unpack(source, target):
        for s in range(R):
            for t in range(T):
                target[s * TILE : (s + 1) * TILE, t * width : (t + 1) * width] = source[
                    s * T + t
                ].astype(F32)

    post(emb_stage, emb_got, 0)
    emb_got[me] = emb_stage[me]
    loads[2].wait()
    gather(cot_ref, cot32, cot_stage)
    post(cot_stage, cot_got, 1)
    cot_got[me] = cot_stage[me]
    for load in loads[6:]:
        load.start()

    for load in loads[3:6]:
        load.wait()
    bounds = []
    total = jnp.int32(0)
    for j in range(seq_ref.shape[2]):
        total = total + seq_ref[0, 0, j]
        bounds.append(total)

    def places(index):
        slot = index // TILE
        place = jnp.zeros_like(index)
        for w in range(1, R):
            place = jnp.where(slot == work_ref[0, 0, w], w, place)
        segment = jnp.zeros_like(index)
        for bound in bounds:
            segment = segment + (place >= bound).astype(jnp.int32)
        return place * TILE + index % TILE, segment

    row_pos, row_seg = places(lax.broadcasted_iota(jnp.int32, (rows, 1), 0))
    lane = lax.broadcasted_iota(jnp.int32, (1, gr), 1)
    col_pos, col_seg = places(lane % rows)
    distance = (row_pos - col_pos).astype(F32)
    allowed = (row_seg == col_seg) & (col_pos <= row_pos)
    slope_s[...] = jnp.where(allowed, distance, -1.0)
    same_head = (
        lax.broadcasted_iota(jnp.int32, (gr, gw), 0) // rows
        == lax.broadcasted_iota(jnp.int32, (gr, gw), 1) // hs
    )
    head_mask = jnp.where(same_head, 1.0, 0.0)
    head_mask16 = head_mask.astype(BF16)

    def spread(block):
        return jnp.concatenate([block] * G, axis=0) * head_mask16

    def collect(full):
        masked = full * head_mask
        total = masked[:rows]
        for h in range(1, G):
            total = total + masked[h * rows : (h + 1) * rows]
        return total

    settle(emb_got, recv_sem.at[0])
    unpack(emb_got, x_s)
    x = x_s[...]
    normal, x_scale = norm_parts(x)
    normed = normal.astype(BF16)
    for load in loads[6:]:
        load.wait()
    projected, slopes_back = [], []
    for c in range(4):
        block = mm(normed, wu[:, c * feat : (c + 1) * feat])
        value, deriv = silu_parts(block)
        projected.append(value if c == 0 else value.astype(BF16))
        slopes_back.append(deriv)
    gate, value, query, key = projected

    relative = slope_s[...]
    allowed = relative >= 0.0
    weights, derivs, pieces, values, keys, queries = [], [], [], [], [], []
    for g in range(H // G):
        cs = slice(g * gw, (g + 1) * gw)
        kd, vd, q = spread(key[:, cs]), spread(value[:, cs]), query[:, cs]
        slope = jnp.zeros((1, gr), F32)
        for h in range(G):
            slope = jnp.where(lane // rows == h, slope_ref[g * G + h], slope)
        scores = mm(q, kd, NT) * scale - slope * relative
        weight, deriv = silu_parts(scores)
        weight = jnp.where(allowed, weight, 0.0).astype(BF16)
        derivs.append(jnp.where(allowed, deriv * scale, 0.0))
        weights.append(weight)
        pieces.append(mm(weight, vd))
        keys.append(kd)
        values.append(vd)
        queries.append(q)
    attended, att_scale = norm_parts(jnp.concatenate(pieces, axis=1))
    gated = (attended * gate).astype(BF16)
    output = x + mm(gated, wo[...])

    scatter(output, out_back)
    post(out_back, out_ret, 2)
    out_own = pltpu.make_async_copy(out_back.at[me], out_ret.at[me], own_sem.at[0])
    out_own.start()

    settle(cot_got, recv_sem.at[1])
    unpack(cot_got, dy_s)
    dy = dy_s[...]
    dgated = mm(dy.astype(BF16), wo[...], NT).astype(BF16).astype(F32)
    dgate = dgated * attended
    datt = norm_back(dgated * gate, attended, att_scale).astype(BF16)
    dv, dq, dk = [], [], []
    for g in range(H // G):
        da = datt[:, g * gw : (g + 1) * gw]
        dw = mm(da, values[g], NT).astype(BF16).astype(F32)
        ds = (dw * derivs[g]).astype(BF16)
        dv.append(collect(mm(weights[g], da, TN)))
        dq.append(mm(ds, keys[g]))
        dk.append(collect(mm(ds, queries[g], TN)))
    dprojected = [dgate] + [
        jnp.concatenate(parts, axis=1).astype(BF16).astype(F32) for parts in (dv, dq, dk)
    ]
    dnormed = jnp.zeros_like(x)
    for c in range(4):
        dz = (dprojected[c] * slopes_back[c]).astype(BF16)
        dnormed = dnormed + mm(dz, wu[:, c * feat : (c + 1) * feat], NT)
    dnormed = dnormed.astype(BF16).astype(F32)
    gradient = norm_back(dnormed, normal, x_scale) + dy

    scatter(gradient, grad_back)
    post(grad_back, grad_ret, 3)
    grad_own = pltpu.make_async_copy(grad_back.at[me], grad_ret.at[me], own_sem.at[1])
    grad_own.start()
    out_own.wait()
    grad_own.wait()
    for index, source in enumerate((emb_stage, cot_stage, out_back, grad_back)):
        settle(source, send_sem.at[index])
    settle(out_ret, recv_sem.at[2])
    settle(grad_ret, recv_sem.at[3])


def fused_shards(
    embeds, cotangent, send_plan, work_plan, sequence_tiles, slopes, uvqk_weight, out_weight
):
    T, R = lax.axis_size("table"), lax.axis_size("replica")
    n, rows, width = T * R, R * TILE, embeds.shape[1]
    feat, H = T * width, slopes.shape[0]
    G = max(1, min(H, MXU // max(feat // H, rows)))
    smem = pl.BlockSpec(memory_space=pltpu.SMEM)
    hbm = pl.BlockSpec(memory_space=pltpu.HBM)
    message = pltpu.VMEM((n, TILE, width), BF16)
    tiles = jax.ShapeDtypeStruct((n, TILE, width), BF16)
    results = pl.pallas_call(
        functools.partial(fused_kernel, T, R, H),
        out_shape=(tiles, tiles),
        in_specs=[hbm] * 8,
        out_specs=(hbm, hbm),
        scratch_shapes=[
            pltpu.SMEM(send_plan.shape, jnp.int32),
            pltpu.SMEM(work_plan.shape, jnp.int32),
            pltpu.SMEM(sequence_tiles.shape, jnp.int32),
            pltpu.SMEM(slopes.shape, F32),
            pltpu.VMEM(embeds.shape, BF16),
            pltpu.VMEM(cotangent.shape, BF16),
            pltpu.VMEM(uvqk_weight.shape, BF16),
            pltpu.VMEM(out_weight.shape, BF16),
            pltpu.VMEM((n, TILE, width), F32),
            pltpu.VMEM((n, TILE, width), F32),
            message,
            message,
            message,
            message,
            pltpu.VMEM((rows, feat), F32),
            pltpu.VMEM((rows, feat), F32),
            pltpu.VMEM((rows, G * rows), F32),
            message,
            message,
            pltpu.SemaphoreType.DMA((8,)),
            pltpu.SemaphoreType.DMA((2,)),
            pltpu.SemaphoreType.DMA((4,)),
            pltpu.SemaphoreType.DMA((4,)),
        ],
        compiler_params=pltpu.CompilerParams(
            collective_id=0, has_side_effects=True, vmem_limit_bytes=VMEM_BYTES
        ),
        name="hstu_fused",
    )(send_plan, work_plan, sequence_tiles, slopes, embeds, cotangent, uvqk_weight, out_weight)
    placed = pl.pallas_call(
        functools.partial(place_kernel, T, R),
        out_shape=(tiles, tiles),
        in_specs=[smem, hbm, hbm],
        out_specs=(hbm, hbm),
        scratch_shapes=[message] * 4 + [pltpu.SemaphoreType.DMA((4,))],
        compiler_params=pltpu.CompilerParams(vmem_limit_bytes=VMEM_BYTES),
        name="place",
    )(send_plan, *results)
    return tuple(part.reshape(embeds.shape) for part in placed)


def place_kernel(
    T, R, send_ref, out_ret, grad_ret, out_home, grad_home, out_got, grad_got, out_put, grad_put, sem
):
    loads = [
        pltpu.make_async_copy(out_ret, out_got, sem.at[0]),
        pltpu.make_async_copy(grad_ret, grad_got, sem.at[1]),
    ]
    stores = [
        pltpu.make_async_copy(out_put, out_home, sem.at[2]),
        pltpu.make_async_copy(grad_put, grad_home, sem.at[3]),
    ]
    for load in loads:
        load.start()
    homes = [[t * R + send_ref[0, t, d] for t in range(T)] for d in range(R)]
    for load, store, got, put in zip(loads, stores, (out_got, grad_got), (out_put, grad_put)):
        load.wait()
        for d in range(R):
            for t in range(T):
                put[homes[d][t]] = got[d * T + t]
        store.start()
    for store in stores:
        store.wait()


def fits_fused(embeds, slopes, T, R):
    width = embeds.shape[1]
    heads = slopes.shape[0]
    row_count = embeds.shape[0] // T
    head_size = width * T // heads
    return (
        width % LANES == 0
        and R % 2 == 0
        and row_count == R * TILE
        and head_size == row_count
        and heads % max(1, min(heads, MXU // head_size)) == 0
    )


def routed(embeds, cotangent, send_plan, work_plan, sequence_tiles, slopes, *weights):
    T, R = lax.axis_size("table"), lax.axis_size("replica")
    body = fused_shards if fits_fused(embeds, slopes, T, R) else shards
    return body(embeds, cotangent, send_plan, work_plan, sequence_tiles, slopes, *weights)


def solution(mesh):
    in_specs = (
        P("replica", "table"),
        P("replica", "table"),
        P("replica", None, None),
        P("replica", "table", None),
        P("replica", "table", None),
        P(),
        P(),
        P(),
    )
    out_specs = (P("replica", "table"), P("replica", "table"))
    return jax.shard_map(routed, mesh=mesh, in_specs=in_specs, out_specs=out_specs, check_vma=False)
```

```python
import functools

import jax
import jax.numpy as jnp
from jax import lax
from jax.experimental import pallas as pl
from jax.experimental.pallas import tpu as pltpu
from jax.sharding import PartitionSpec as P

MESH = pl.DeviceIdType.MESH
MXU = 256
LANES = 128
VMEM_BYTES = 64 << 20
F32 = jnp.float32
BF16 = jnp.bfloat16

TILE = 8


EPSILON = 1e-05


def layer_norm(features):
    centre = jnp.mean(features, axis=-1, keepdims=True)
    centred = features - centre
    spread = jnp.mean(centred * centred, axis=-1, keepdims=True)
    return centred * lax.rsqrt(spread + EPSILON)


def segment_ids(lengths, row_count, tile_rows):
    boundary = jnp.cumsum(lengths)
    tile_index = jnp.arange(row_count, dtype=jnp.int32) // tile_rows
    return jnp.sum((tile_index[None, :] >= boundary[:, None]).astype(jnp.int32), axis=0)


def hstu_layer(inputs, segment, slopes, uvqk_weight, out_weight):
    row_count, feature_count = inputs.shape
    head_count = slopes.shape[0]
    head_size = feature_count // head_count
    score_scale = head_size ** (-0.5)
    normed = layer_norm(inputs.astype(jnp.float32)).astype(jnp.bfloat16)
    projected = jax.nn.silu(jnp.dot(normed, uvqk_weight, preferred_element_type=jnp.float32))
    gate_part = projected[:, :feature_count]
    value_part = projected[:, feature_count : 2 * feature_count].astype(jnp.bfloat16)
    query_part = projected[:, 2 * feature_count : 3 * feature_count].astype(jnp.bfloat16)
    key_part = projected[:, 3 * feature_count :].astype(jnp.bfloat16)
    row_index = lax.broadcasted_iota(jnp.int32, (row_count, row_count), 0)
    col_index = lax.broadcasted_iota(jnp.int32, (row_count, row_count), 1)
    allowed = (segment[:, None] == segment[None, :]) & (col_index <= row_index)
    distance = (row_index - col_index).astype(jnp.float32)
    pieces = []
    for head_index in range(head_count):
        lower = head_index * head_size
        upper = lower + head_size
        scores = jnp.dot(
            query_part[:, lower:upper],
            key_part[:, lower:upper].T,
            preferred_element_type=jnp.float32,
        )
        scores = scores * score_scale - slopes[head_index] * distance
        weights = jnp.where(allowed, jax.nn.silu(scores), jnp.zeros_like(scores)).astype(
            jnp.bfloat16
        )
        pieces.append(
            jnp.dot(weights, value_part[:, lower:upper], preferred_element_type=jnp.float32)
        )
    attended = jnp.concatenate(pieces, axis=1)
    gated = (layer_norm(attended) * gate_part).astype(jnp.bfloat16)
    mixing = jnp.dot(gated, out_weight, preferred_element_type=jnp.float32)
    return (inputs.astype(jnp.float32) + mixing).astype(jnp.bfloat16)


def forward_backward(inputs, grad_rows, segment, slopes, uvqk_weight, out_weight):

    def apply_layer(layer_input):
        return hstu_layer(layer_input, segment, slopes, uvqk_weight, out_weight)

    outputs, pullback = jax.vjp(apply_layer, inputs)
    return (outputs, pullback(grad_rows)[0])


def shards(
    embeds, cotangent, send_plan, work_plan, sequence_tiles, slopes, uvqk_weight, out_weight
):
    table_count = lax.axis_size("table")
    replica_count = lax.axis_size("replica")
    column_count = embeds.shape[1]
    row_count = embeds.shape[0] // table_count
    tile_count = row_count // TILE
    peer_rows = row_count // replica_count
    feature_count = column_count * table_count
    block_plans = send_plan[0]
    own_send = lax.dynamic_index_in_dim(block_plans, lax.axis_index("table"), 0, keepdims=False)
    own_work = work_plan[0, 0]
    segment = segment_ids(sequence_tiles[0, 0], row_count, TILE)
    tile_order = jnp.arange(tile_count, dtype=jnp.int32)
    row_inputs, row_grads = (
        lax.all_to_all(embeds, "table", split_axis=0, concat_axis=1, tiled=True),
        lax.all_to_all(cotangent, "table", split_axis=0, concat_axis=1, tiled=True),
    )

    def to_slots(shard_rows):
        tiled = shard_rows.reshape(tile_count, TILE, feature_count)
        return tiled[own_send]

    got_inputs, got_grads = (
        lax.all_to_all(to_slots(row_inputs), "replica", split_axis=0, concat_axis=0, tiled=True),
        lax.all_to_all(to_slots(row_grads), "replica", split_axis=0, concat_axis=0, tiled=True),
    )
    work_inputs = got_inputs[own_work].reshape(row_count, feature_count)
    work_grads = got_grads[own_work].reshape(row_count, feature_count)
    outputs, gradient = forward_backward(
        work_inputs, work_grads, segment, slopes, uvqk_weight, out_weight
    )
    undo_work = jnp.zeros((tile_count,), jnp.int32).at[own_work].set(tile_order)

    def to_sources(result):
        return result.reshape(tile_count, TILE, feature_count)[undo_work]

    slot_outputs = to_sources(outputs)
    slot_grads = to_sources(gradient)
    back_outputs, back_grads = (
        lax.all_to_all(slot_outputs, "replica", split_axis=0, concat_axis=0, tiled=True),
        lax.all_to_all(slot_grads, "replica", split_axis=0, concat_axis=0, tiled=True),
    )
    undo_send = jnp.zeros((tile_count,), jnp.int32).at[own_send].set(tile_order)

    def to_home(result):
        return result[undo_send].reshape(row_count, feature_count)

    layer_output, input_gradient = (
        lax.all_to_all(to_home(back_outputs), "table", split_axis=1, concat_axis=0, tiled=True),
        lax.all_to_all(to_home(back_grads), "table", split_axis=1, concat_axis=0, tiled=True),
    )
    return (layer_output, input_gradient)


NT = (((1,), (1,)), ((), ()))
TN = (((0,), (0,)), ((), ()))


def mm(a, b, dims=(((1,), (0,)), ((), ()))):
    return lax.dot_general(a, b, dims, preferred_element_type=F32)


def norm_parts(features):
    centred = features - jnp.mean(features, axis=-1, keepdims=True)
    scale = lax.rsqrt(jnp.mean(centred * centred, axis=-1, keepdims=True) + EPSILON)
    return centred * scale, scale


def norm_back(grad, normal, scale):
    along = jnp.mean(grad * normal, axis=-1, keepdims=True)
    return scale * (grad - jnp.mean(grad, axis=-1, keepdims=True) - normal * along)


def silu_parts(v):
    sig = 0.5 * jnp.tanh(0.5 * v) + 0.5
    value = v * sig
    return value, sig + value * (1.0 - sig)


def fused_kernel(
    T, R, H,
    send_hbm, work_hbm, seq_hbm, slope_hbm, emb_hbm, cot_hbm, wu_hbm, wo_hbm,
    ret,
    send_ref, work_ref, seq_ref, slope_ref, emb_ref, cot_ref,
    wu, wo, emb_stage, cot_stage, emb_got, cot_got, x_s, dy_s, slope_s,
    out_back, grad_back,
    in_sem, own_sem, send_sem, recv_sem,
):
    n = T * R
    rows = R * TILE
    width = emb_ref.shape[2]
    feat = T * width
    hs = feat // H
    G = max(1, min(H, MXU // max(hs, rows)))
    gw, gr = G * hs, G * rows
    scale = hs ** (-0.5)
    me_t = lax.axis_index("table")
    me_r = lax.axis_index("replica")
    me = me_r * T + me_t

    sources = (send_hbm, emb_hbm, cot_hbm, work_hbm, seq_hbm, slope_hbm, wu_hbm, wo_hbm)
    targets = (send_ref, emb_ref, cot_ref, work_ref, seq_ref, slope_ref, wu, wo)
    loads = [
        pltpu.make_async_copy(source, target, in_sem.at[i])
        for i, (source, target) in enumerate(zip(sources, targets))
    ]
    for load in loads[:6]:
        load.start()

    def partner(own, step, count):
        other, bit = jnp.int32(0), 1
        while bit < count:
            held = lax.rem(lax.div(own, bit), 2)
            other = other + bit * (1 - held if step & bit else held)
            bit = 2 * bit
        return other

    peers = []
    for far in range(R - 1, -1, -1):
        for near in range(T - 1, -1, -1):
            if far or near:
                t, r = partner(me_t, near, T), partner(me_r, far, R)
                peers.append((r * T + t, {"table": t, "replica": r}))

    barrier = pltpu.get_barrier_semaphore()
    for _, device in peers:
        pl.semaphore_signal(barrier, inc=1, device_id=device, device_id_type=MESH)

    def gather(source, target):
        for d in range(R):
            for t in range(T):
                target[d * T + t] = source[t * R + send_ref[0, t, d]]

    loads[0].wait()
    loads[1].wait()
    gather(emb_ref, emb_stage)
    pl.semaphore_wait(barrier, n - 1)

    def post(src, dst, index, base=0):
        for other, device in peers:
            pltpu.make_async_remote_copy(
                src_ref=src.at[other],
                dst_ref=dst.at[base + me],
                send_sem=send_sem.at[index],
                recv_sem=recv_sem.at[index],
                device_id=device,
                device_id_type=MESH,
            ).start()

    def settle(ref, sem):
        part = ref.at[pl.ds(0, n - 1)]
        pltpu.make_async_copy(part, part, sem).wait()

    def scatter(source, target):
        for s in range(R):
            for t in range(T):
                target[s * T + t] = source[
                    s * TILE : (s + 1) * TILE, t * width : (t + 1) * width
                ].astype(BF16)

    def unpack(source, target):
        for s in range(R):
            for t in range(T):
                target[s * TILE : (s + 1) * TILE, t * width : (t + 1) * width] = source[
                    s * T + t
                ].astype(F32)

    post(emb_stage, emb_got, 0)
    emb_got[me] = emb_stage[me]
    loads[2].wait()
    gather(cot_ref, cot_stage)
    post(cot_stage, cot_got, 1)
    cot_got[me] = cot_stage[me]
    for load in loads[6:]:
        load.start()

    for load in loads[3:6]:
        load.wait()
    bounds = []
    total = jnp.int32(0)
    for j in range(seq_ref.shape[2]):
        total = total + seq_ref[0, 0, j]
        bounds.append(total)

    def places(index):
        slot = index // TILE
        place = jnp.zeros_like(index)
        for w in range(1, R):
            place = jnp.where(slot == work_ref[0, 0, w], w, place)
        segment = jnp.zeros_like(index)
        for bound in bounds:
            segment = segment + (place >= bound).astype(jnp.int32)
        return place * TILE + index % TILE, segment

    row_pos, row_seg = places(lax.broadcasted_iota(jnp.int32, (rows, 1), 0))
    lane = lax.broadcasted_iota(jnp.int32, (1, gr), 1)
    col_pos, col_seg = places(lane % rows)
    distance = (row_pos - col_pos).astype(F32)
    allowed = (row_seg == col_seg) & (col_pos <= row_pos)
    slope_s[...] = jnp.where(allowed, distance, -1.0)
    same_head = (
        lax.broadcasted_iota(jnp.int32, (gr, gw), 0) // rows
        == lax.broadcasted_iota(jnp.int32, (gr, gw), 1) // hs
    )
    head_mask = jnp.where(same_head, 1.0, 0.0)
    head_mask16 = head_mask.astype(BF16)

    def spread(block):
        return jnp.concatenate([block] * G, axis=0) * head_mask16

    def collect(full):
        masked = full * head_mask
        total = masked[:rows]
        for h in range(1, G):
            total = total + masked[h * rows : (h + 1) * rows]
        return total

    settle(emb_got, recv_sem.at[0])
    unpack(emb_got, x_s)
    x = x_s[...]
    normal, x_scale = norm_parts(x)
    normed = normal.astype(BF16)
    for load in loads[6:]:
        load.wait()
    projected, slopes_back = [], []
    for c in range(4):
        block = mm(normed, wu[:, c * feat : (c + 1) * feat])
        value, deriv = silu_parts(block)
        projected.append(value if c == 0 else value.astype(BF16))
        slopes_back.append(deriv)
    gate, value, query, key = projected

    relative = slope_s[...]
    allowed = relative >= 0.0
    weights, derivs, pieces, values, keys, queries = [], [], [], [], [], []
    for g in range(H // G):
        cs = slice(g * gw, (g + 1) * gw)
        kd, vd, q = spread(key[:, cs]), spread(value[:, cs]), query[:, cs]
        slope = jnp.zeros((1, gr), F32)
        for h in range(G):
            slope = jnp.where(lane // rows == h, slope_ref[g * G + h], slope)
        scores = mm(q, kd, NT) * scale - slope * relative
        weight, deriv = silu_parts(scores)
        weight = jnp.where(allowed, weight, 0.0).astype(BF16)
        derivs.append(jnp.where(allowed, deriv * scale, 0.0))
        weights.append(weight)
        pieces.append(mm(weight, vd))
        keys.append(kd)
        values.append(vd)
        queries.append(q)
    attended, att_scale = norm_parts(jnp.concatenate(pieces, axis=1))
    gated = (attended * gate).astype(BF16)
    output = x + mm(gated, wo[...])

    scatter(output, out_back)
    post(out_back, ret, 2)
    out_own = pltpu.make_async_copy(out_back.at[me], ret.at[me], own_sem.at[0])
    out_own.start()

    settle(cot_got, recv_sem.at[1])
    unpack(cot_got, dy_s)
    dy = dy_s[...]
    dgated = mm(dy.astype(BF16), wo[...], NT).astype(BF16).astype(F32)
    dgate = dgated * attended
    datt = norm_back(dgated * gate, attended, att_scale).astype(BF16)
    dv, dq, dk = [], [], []
    for g in range(H // G):
        da = datt[:, g * gw : (g + 1) * gw]
        dw = mm(da, values[g], NT).astype(BF16).astype(F32)
        ds = (dw * derivs[g]).astype(BF16)
        dv.append(collect(mm(weights[g], da, TN)))
        dq.append(mm(ds, keys[g]))
        dk.append(collect(mm(ds, queries[g], TN)))
    dprojected = [dgate] + [
        jnp.concatenate(parts, axis=1).astype(BF16).astype(F32) for parts in (dv, dq, dk)
    ]
    dnormed = jnp.zeros_like(x)
    for c in range(4):
        dz = (dprojected[c] * slopes_back[c]).astype(BF16)
        dnormed = dnormed + mm(dz, wu[:, c * feat : (c + 1) * feat], NT)
    dnormed = dnormed.astype(BF16).astype(F32)
    gradient = norm_back(dnormed, normal, x_scale) + dy

    scatter(gradient, grad_back)
    post(grad_back, ret, 3, n)
    grad_own = pltpu.make_async_copy(grad_back.at[me], ret.at[n + me], own_sem.at[1])
    grad_own.start()
    out_own.wait()
    grad_own.wait()
    for index, source in enumerate((emb_stage, cot_stage, out_back, grad_back)):
        settle(source, send_sem.at[index])
    settle(out_back, recv_sem.at[2])
    settle(grad_back, recv_sem.at[3])


def fused_shards(
    embeds, cotangent, send_plan, work_plan, sequence_tiles, slopes, uvqk_weight, out_weight
):
    T, R = lax.axis_size("table"), lax.axis_size("replica")
    n, rows, width = T * R, R * TILE, embeds.shape[1]
    feat, H = T * width, slopes.shape[0]
    G = max(1, min(H, MXU // max(feat // H, rows)))
    vmem = pl.BlockSpec(memory_space=pltpu.VMEM)
    smem = pl.BlockSpec(memory_space=pltpu.SMEM)
    hbm = pl.BlockSpec(memory_space=pltpu.HBM)
    message = pltpu.VMEM((n, TILE, width), BF16)
    tiles = jax.ShapeDtypeStruct((n, TILE, width), BF16)
    ret = pl.pallas_call(
        functools.partial(fused_kernel, T, R, H),
        out_shape=jax.ShapeDtypeStruct((2 * n, TILE, width), BF16),
        in_specs=[hbm] * 8,
        out_specs=hbm,
        scratch_shapes=[
            pltpu.SMEM(send_plan.shape, jnp.int32),
            pltpu.SMEM(work_plan.shape, jnp.int32),
            pltpu.SMEM(sequence_tiles.shape, jnp.int32),
            pltpu.SMEM(slopes.shape, F32),
            message,
            message,
            pltpu.VMEM(uvqk_weight.shape, BF16),
            pltpu.VMEM(out_weight.shape, BF16),
            message,
            message,
            message,
            message,
            pltpu.VMEM((rows, feat), F32),
            pltpu.VMEM((rows, feat), F32),
            pltpu.VMEM((rows, G * rows), F32),
            message,
            message,
            pltpu.SemaphoreType.DMA((8,)),
            pltpu.SemaphoreType.DMA((2,)),
            pltpu.SemaphoreType.DMA((4,)),
            pltpu.SemaphoreType.DMA((4,)),
        ],
        compiler_params=pltpu.CompilerParams(
            collective_id=0, has_side_effects=True, vmem_limit_bytes=VMEM_BYTES
        ),
        name="hstu_fused",
    )(
        send_plan,
        work_plan,
        sequence_tiles,
        slopes,
        embeds.reshape(tiles.shape),
        cotangent.reshape(tiles.shape),
        uvqk_weight,
        out_weight,
    )
    placed = pl.pallas_call(
        functools.partial(place_kernel, T, R),
        out_shape=(tiles, tiles),
        in_specs=[smem, vmem],
        out_specs=(vmem, vmem),
        compiler_params=pltpu.CompilerParams(vmem_limit_bytes=VMEM_BYTES),
        name="place",
    )(send_plan, ret)
    return tuple(part.reshape(embeds.shape) for part in placed)


def place_kernel(T, R, send_ref, ret_ref, out_ref, grad_ref):
    for t in range(T):
        for d in range(R):
            home = t * R + send_ref[0, t, d]
            out_ref[home] = ret_ref[d * T + t]
            grad_ref[home] = ret_ref[T * R + d * T + t]


def fits_fused(embeds, slopes, T, R):
    width = embeds.shape[1]
    heads = slopes.shape[0]
    row_count = embeds.shape[0] // T
    head_size = width * T // heads
    return (
        width % LANES == 0
        and R & (R - 1) == 0
        and T & (T - 1) == 0
        and row_count == R * TILE
        and head_size == row_count
        and heads % max(1, min(heads, MXU // head_size)) == 0
    )


def routed(embeds, cotangent, send_plan, work_plan, sequence_tiles, slopes, *weights):
    T, R = lax.axis_size("table"), lax.axis_size("replica")
    body = fused_shards if fits_fused(embeds, slopes, T, R) else shards
    return body(embeds, cotangent, send_plan, work_plan, sequence_tiles, slopes, *weights)


def solution(mesh):
    in_specs = (
        P("replica", "table"),
        P("replica", "table"),
        P("replica", None, None),
        P("replica", "table", None),
        P("replica", "table", None),
        P(),
        P(),
        P(),
    )
    out_specs = (P("replica", "table"), P("replica", "table"))
    return jax.shard_map(routed, mesh=mesh, in_specs=in_specs, out_specs=out_specs, check_vma=False)
```

```python
import functools

import jax
import jax.numpy as jnp
from jax import lax
from jax.experimental import pallas as pl
from jax.experimental.pallas import tpu as pltpu
from jax.sharding import PartitionSpec as P

MESH = pl.DeviceIdType.MESH
MXU = 256
LANES = 128
VMEM_BYTES = 64 << 20
F32 = jnp.float32
BF16 = jnp.bfloat16

TILE = 8


EPSILON = 1e-05


def layer_norm(features):
    centre = jnp.mean(features, axis=-1, keepdims=True)
    centred = features - centre
    spread = jnp.mean(centred * centred, axis=-1, keepdims=True)
    return centred * lax.rsqrt(spread + EPSILON)


def segment_ids(lengths, row_count, tile_rows):
    boundary = jnp.cumsum(lengths)
    tile_index = jnp.arange(row_count, dtype=jnp.int32) // tile_rows
    return jnp.sum((tile_index[None, :] >= boundary[:, None]).astype(jnp.int32), axis=0)


def hstu_layer(inputs, segment, slopes, uvqk_weight, out_weight):
    row_count, feature_count = inputs.shape
    head_count = slopes.shape[0]
    head_size = feature_count // head_count
    score_scale = head_size ** (-0.5)
    normed = layer_norm(inputs.astype(jnp.float32)).astype(jnp.bfloat16)
    projected = jax.nn.silu(jnp.dot(normed, uvqk_weight, preferred_element_type=jnp.float32))
    gate_part = projected[:, :feature_count]
    value_part = projected[:, feature_count : 2 * feature_count].astype(jnp.bfloat16)
    query_part = projected[:, 2 * feature_count : 3 * feature_count].astype(jnp.bfloat16)
    key_part = projected[:, 3 * feature_count :].astype(jnp.bfloat16)
    row_index = lax.broadcasted_iota(jnp.int32, (row_count, row_count), 0)
    col_index = lax.broadcasted_iota(jnp.int32, (row_count, row_count), 1)
    allowed = (segment[:, None] == segment[None, :]) & (col_index <= row_index)
    distance = (row_index - col_index).astype(jnp.float32)
    pieces = []
    for head_index in range(head_count):
        lower = head_index * head_size
        upper = lower + head_size
        scores = jnp.dot(
            query_part[:, lower:upper],
            key_part[:, lower:upper].T,
            preferred_element_type=jnp.float32,
        )
        scores = scores * score_scale - slopes[head_index] * distance
        weights = jnp.where(allowed, jax.nn.silu(scores), jnp.zeros_like(scores)).astype(
            jnp.bfloat16
        )
        pieces.append(
            jnp.dot(weights, value_part[:, lower:upper], preferred_element_type=jnp.float32)
        )
    attended = jnp.concatenate(pieces, axis=1)
    gated = (layer_norm(attended) * gate_part).astype(jnp.bfloat16)
    mixing = jnp.dot(gated, out_weight, preferred_element_type=jnp.float32)
    return (inputs.astype(jnp.float32) + mixing).astype(jnp.bfloat16)


def forward_backward(inputs, grad_rows, segment, slopes, uvqk_weight, out_weight):

    def apply_layer(layer_input):
        return hstu_layer(layer_input, segment, slopes, uvqk_weight, out_weight)

    outputs, pullback = jax.vjp(apply_layer, inputs)
    return (outputs, pullback(grad_rows)[0])


def shards(
    embeds, cotangent, send_plan, work_plan, sequence_tiles, slopes, uvqk_weight, out_weight
):
    table_count = lax.axis_size("table")
    replica_count = lax.axis_size("replica")
    column_count = embeds.shape[1]
    row_count = embeds.shape[0] // table_count
    tile_count = row_count // TILE
    peer_rows = row_count // replica_count
    feature_count = column_count * table_count
    block_plans = send_plan[0]
    own_send = lax.dynamic_index_in_dim(block_plans, lax.axis_index("table"), 0, keepdims=False)
    own_work = work_plan[0, 0]
    segment = segment_ids(sequence_tiles[0, 0], row_count, TILE)
    tile_order = jnp.arange(tile_count, dtype=jnp.int32)
    row_inputs, row_grads = (
        lax.all_to_all(embeds, "table", split_axis=0, concat_axis=1, tiled=True),
        lax.all_to_all(cotangent, "table", split_axis=0, concat_axis=1, tiled=True),
    )

    def to_slots(shard_rows):
        tiled = shard_rows.reshape(tile_count, TILE, feature_count)
        return tiled[own_send]

    got_inputs, got_grads = (
        lax.all_to_all(to_slots(row_inputs), "replica", split_axis=0, concat_axis=0, tiled=True),
        lax.all_to_all(to_slots(row_grads), "replica", split_axis=0, concat_axis=0, tiled=True),
    )
    work_inputs = got_inputs[own_work].reshape(row_count, feature_count)
    work_grads = got_grads[own_work].reshape(row_count, feature_count)
    outputs, gradient = forward_backward(
        work_inputs, work_grads, segment, slopes, uvqk_weight, out_weight
    )
    undo_work = jnp.zeros((tile_count,), jnp.int32).at[own_work].set(tile_order)

    def to_sources(result):
        return result.reshape(tile_count, TILE, feature_count)[undo_work]

    slot_outputs = to_sources(outputs)
    slot_grads = to_sources(gradient)
    back_outputs, back_grads = (
        lax.all_to_all(slot_outputs, "replica", split_axis=0, concat_axis=0, tiled=True),
        lax.all_to_all(slot_grads, "replica", split_axis=0, concat_axis=0, tiled=True),
    )
    undo_send = jnp.zeros((tile_count,), jnp.int32).at[own_send].set(tile_order)

    def to_home(result):
        return result[undo_send].reshape(row_count, feature_count)

    layer_output, input_gradient = (
        lax.all_to_all(to_home(back_outputs), "table", split_axis=1, concat_axis=0, tiled=True),
        lax.all_to_all(to_home(back_grads), "table", split_axis=1, concat_axis=0, tiled=True),
    )
    return (layer_output, input_gradient)


NT = (((1,), (1,)), ((), ()))
TN = (((0,), (0,)), ((), ()))


def mm(a, b, dims=(((1,), (0,)), ((), ()))):
    return lax.dot_general(a, b, dims, preferred_element_type=F32)


def norm_parts(features):
    centred = features - jnp.mean(features, axis=-1, keepdims=True)
    scale = lax.rsqrt(jnp.mean(centred * centred, axis=-1, keepdims=True) + EPSILON)
    return centred * scale, scale


def norm_back(grad, normal, scale):
    along = jnp.mean(grad * normal, axis=-1, keepdims=True)
    return scale * (grad - jnp.mean(grad, axis=-1, keepdims=True) - normal * along)


def silu_parts(v):
    sig = 0.5 * jnp.tanh(0.5 * v) + 0.5
    value = v * sig
    return value, sig + value * (1.0 - sig)


def fused_kernel(
    T, R, H,
    send_hbm, work_hbm, seq_hbm, slope_hbm, emb_hbm, cot_hbm, wu_hbm, wo_hbm,
    ret,
    send_ref, work_ref, seq_ref, slope_ref, emb_ref, cot_ref,
    wu, wo, emb_stage, cot_stage, emb_got, cot_got, x_s, dy_s, slope_s,
    out_back, grad_back,
    in_sem, own_sem, send_sem, recv_sem,
):
    n = T * R
    rows = R * TILE
    width = emb_ref.shape[2]
    feat = T * width
    hs = feat // H
    G = max(1, min(H, MXU // max(hs, rows)))
    gw, gr = G * hs, G * rows
    scale = hs ** (-0.5)
    me_t = lax.axis_index("table")
    me_r = lax.axis_index("replica")
    me = me_r * T + me_t

    sources = (send_hbm, emb_hbm, cot_hbm, work_hbm, seq_hbm, slope_hbm, wu_hbm, wo_hbm)
    targets = (send_ref, emb_ref, cot_ref, work_ref, seq_ref, slope_ref, wu, wo)
    loads = [
        pltpu.make_async_copy(source, target, in_sem.at[i])
        for i, (source, target) in enumerate(zip(sources, targets))
    ]
    for load in loads[:6]:
        load.start()

    def partner(own, step, count):
        other, bit = jnp.int32(0), 1
        while bit < count:
            held = lax.rem(lax.div(own, bit), 2)
            other = other + bit * (1 - held if step & bit else held)
            bit = 2 * bit
        return other

    peers = []
    for far in range(R - 1, -1, -1):
        for near in range(T - 1, -1, -1):
            if far or near:
                t, r = partner(me_t, near, T), partner(me_r, far, R)
                peers.append((r * T + t, {"table": t, "replica": r}))

    barrier = pltpu.get_barrier_semaphore()
    for _, device in peers:
        pl.semaphore_signal(barrier, inc=1, device_id=device, device_id_type=MESH)

    def gather(source, target):
        for d in range(R):
            for t in range(T):
                target[d * T + t] = source[t * R + send_ref[0, t, d]]

    loads[0].wait()
    loads[1].wait()
    gather(emb_ref, emb_stage)
    pl.semaphore_wait(barrier, n - 1)

    def post(src, dst, index, base=0):
        for other, device in peers:
            pltpu.make_async_remote_copy(
                src_ref=src.at[other],
                dst_ref=dst.at[base + me],
                send_sem=send_sem.at[index],
                recv_sem=recv_sem.at[index],
                device_id=device,
                device_id_type=MESH,
            ).start()

    def settle(ref, sem):
        part = ref.at[pl.ds(0, n - 1)]
        pltpu.make_async_copy(part, part, sem).wait()

    def scatter(source, target):
        for s in range(R):
            for t in range(T):
                target[s * T + t] = source[
                    s * TILE : (s + 1) * TILE, t * width : (t + 1) * width
                ].astype(BF16)

    def unpack(source, target):
        for s in range(R):
            for t in range(T):
                target[s * TILE : (s + 1) * TILE, t * width : (t + 1) * width] = source[
                    s * T + t
                ].astype(F32)

    post(emb_stage, emb_got, 0)
    emb_got[me] = emb_stage[me]
    loads[2].wait()
    gather(cot_ref, cot_stage)
    post(cot_stage, cot_got, 1)
    cot_got[me] = cot_stage[me]
    for load in loads[6:]:
        load.start()

    for load in loads[3:6]:
        load.wait()
    bounds = []
    total = jnp.int32(0)
    for j in range(seq_ref.shape[2]):
        total = total + seq_ref[0, 0, j]
        bounds.append(total)

    def places(index):
        slot = index // TILE
        place = jnp.zeros_like(index)
        for w in range(1, R):
            place = jnp.where(slot == work_ref[0, 0, w], w, place)
        segment = jnp.zeros_like(index)
        for bound in bounds:
            segment = segment + (place >= bound).astype(jnp.int32)
        return place * TILE + index % TILE, segment

    row_pos, row_seg = places(lax.broadcasted_iota(jnp.int32, (rows, 1), 0))
    lane = lax.broadcasted_iota(jnp.int32, (1, gr), 1)
    col_pos, col_seg = places(lane % rows)
    distance = (row_pos - col_pos).astype(F32)
    allowed = (row_seg == col_seg) & (col_pos <= row_pos)
    slope_s[...] = jnp.where(allowed, distance, -1.0)
    same_head = (
        lax.broadcasted_iota(jnp.int32, (gr, gw), 0) // rows
        == lax.broadcasted_iota(jnp.int32, (gr, gw), 1) // hs
    )
    head_mask = jnp.where(same_head, 1.0, 0.0)
    head_mask16 = head_mask.astype(BF16)

    def spread(block):
        return jnp.concatenate([block] * G, axis=0) * head_mask16

    def collect(full):
        masked = full * head_mask
        total = masked[:rows]
        for h in range(1, G):
            total = total + masked[h * rows : (h + 1) * rows]
        return total

    settle(emb_got, recv_sem.at[0])
    unpack(emb_got, x_s)
    x = x_s[...]
    normal, x_scale = norm_parts(x)
    normed = normal.astype(BF16)
    for load in loads[6:]:
        load.wait()
    projected, slopes_back = [], []
    for c in range(4):
        block = mm(normed, wu[:, c * feat : (c + 1) * feat])
        value, deriv = silu_parts(block)
        projected.append(value if c == 0 else value.astype(BF16))
        slopes_back.append(deriv)
    gate, value, query, key = projected

    settle(cot_got, recv_sem.at[1])
    unpack(cot_got, dy_s)
    dy = dy_s[...]
    dgated = mm(dy.astype(BF16), wo[...], NT).astype(BF16).astype(F32)

    relative = slope_s[...]
    allowed = relative >= 0.0
    weights, derivs, pieces, values, keys, queries = [], [], [], [], [], []
    for g in range(H // G):
        cs = slice(g * gw, (g + 1) * gw)
        kd, vd, q = spread(key[:, cs]), spread(value[:, cs]), query[:, cs]
        slope = jnp.zeros((1, gr), F32)
        for h in range(G):
            slope = jnp.where(lane // rows == h, slope_ref[g * G + h], slope)
        scores = mm(q, kd, NT) * scale - slope * relative
        weight, deriv = silu_parts(scores)
        weight = jnp.where(allowed, weight, 0.0).astype(BF16)
        derivs.append(jnp.where(allowed, deriv * scale, 0.0))
        weights.append(weight)
        pieces.append(mm(weight, vd))
        keys.append(kd)
        values.append(vd)
        queries.append(q)
    attended, att_scale = norm_parts(jnp.concatenate(pieces, axis=1))
    dgate = dgated * attended
    datt = norm_back(dgated * gate, attended, att_scale).astype(BF16)
    gated = (attended * gate).astype(BF16)
    output = x + mm(gated, wo[...])
    scatter(output, out_back)
    dv, dq, dk = [], [], []
    for g in range(H // G):
        da = datt[:, g * gw : (g + 1) * gw]
        dw = mm(da, values[g], NT).astype(BF16).astype(F32)
        ds = (dw * derivs[g]).astype(BF16)
        dv.append(collect(mm(weights[g], da, TN)))
        dq.append(mm(ds, keys[g]))
        dk.append(collect(mm(ds, queries[g], TN)))
    post(out_back, ret, 2)
    out_own = pltpu.make_async_copy(out_back.at[me], ret.at[me], own_sem.at[0])
    out_own.start()
    dprojected = [dgate] + [
        jnp.concatenate(parts, axis=1).astype(BF16).astype(F32) for parts in (dv, dq, dk)
    ]
    dnormed = jnp.zeros_like(x)
    for c in range(4):
        dz = (dprojected[c] * slopes_back[c]).astype(BF16)
        dnormed = dnormed + mm(dz, wu[:, c * feat : (c + 1) * feat], NT)
    dnormed = dnormed.astype(BF16).astype(F32)
    gradient = norm_back(dnormed, normal, x_scale) + dy

    scatter(gradient, grad_back)
    post(grad_back, ret, 3, n)
    grad_own = pltpu.make_async_copy(grad_back.at[me], ret.at[n + me], own_sem.at[1])
    grad_own.start()
    out_own.wait()
    grad_own.wait()
    for index, source in enumerate((emb_stage, cot_stage, out_back, grad_back)):
        settle(source, send_sem.at[index])
    settle(out_back, recv_sem.at[2])
    settle(grad_back, recv_sem.at[3])


def fused_shards(
    embeds, cotangent, send_plan, work_plan, sequence_tiles, slopes, uvqk_weight, out_weight
):
    T, R = lax.axis_size("table"), lax.axis_size("replica")
    n, rows, width = T * R, R * TILE, embeds.shape[1]
    feat, H = T * width, slopes.shape[0]
    G = max(1, min(H, MXU // max(feat // H, rows)))
    vmem = pl.BlockSpec(memory_space=pltpu.VMEM)
    smem = pl.BlockSpec(memory_space=pltpu.SMEM)
    hbm = pl.BlockSpec(memory_space=pltpu.HBM)
    message = pltpu.VMEM((n, TILE, width), BF16)
    tiles = jax.ShapeDtypeStruct((n, TILE, width), BF16)
    ret = pl.pallas_call(
        functools.partial(fused_kernel, T, R, H),
        out_shape=jax.ShapeDtypeStruct((2 * n, TILE, width), BF16),
        in_specs=[hbm] * 8,
        out_specs=hbm,
        scratch_shapes=[
            pltpu.SMEM(send_plan.shape, jnp.int32),
            pltpu.SMEM(work_plan.shape, jnp.int32),
            pltpu.SMEM(sequence_tiles.shape, jnp.int32),
            pltpu.SMEM(slopes.shape, F32),
            message,
            message,
            pltpu.VMEM(uvqk_weight.shape, BF16),
            pltpu.VMEM(out_weight.shape, BF16),
            message,
            message,
            message,
            message,
            pltpu.VMEM((rows, feat), F32),
            pltpu.VMEM((rows, feat), F32),
            pltpu.VMEM((rows, G * rows), F32),
            message,
            message,
            pltpu.SemaphoreType.DMA((8,)),
            pltpu.SemaphoreType.DMA((2,)),
            pltpu.SemaphoreType.DMA((4,)),
            pltpu.SemaphoreType.DMA((4,)),
        ],
        compiler_params=pltpu.CompilerParams(
            collective_id=0, has_side_effects=True, vmem_limit_bytes=VMEM_BYTES
        ),
        name="hstu_fused",
    )(
        send_plan,
        work_plan,
        sequence_tiles,
        slopes,
        embeds.reshape(tiles.shape),
        cotangent.reshape(tiles.shape),
        uvqk_weight,
        out_weight,
    )
    placed = pl.pallas_call(
        functools.partial(place_kernel, T, R),
        out_shape=(tiles, tiles),
        in_specs=[smem, vmem],
        out_specs=(vmem, vmem),
        compiler_params=pltpu.CompilerParams(vmem_limit_bytes=VMEM_BYTES),
        name="place",
    )(send_plan, ret)
    return tuple(part.reshape(embeds.shape) for part in placed)


def place_kernel(T, R, send_ref, ret_ref, out_ref, grad_ref):
    for t in range(T):
        for d in range(R):
            home = t * R + send_ref[0, t, d]
            out_ref[home] = ret_ref[d * T + t]
            grad_ref[home] = ret_ref[T * R + d * T + t]


def fits_fused(embeds, slopes, T, R):
    width = embeds.shape[1]
    heads = slopes.shape[0]
    row_count = embeds.shape[0] // T
    head_size = width * T // heads
    return (
        width % LANES == 0
        and R & (R - 1) == 0
        and T & (T - 1) == 0
        and row_count == R * TILE
        and head_size == row_count
        and heads % max(1, min(heads, MXU // head_size)) == 0
    )


def routed(embeds, cotangent, send_plan, work_plan, sequence_tiles, slopes, *weights):
    T, R = lax.axis_size("table"), lax.axis_size("replica")
    body = fused_shards if fits_fused(embeds, slopes, T, R) else shards
    return body(embeds, cotangent, send_plan, work_plan, sequence_tiles, slopes, *weights)


def solution(mesh):
    in_specs = (
        P("replica", "table"),
        P("replica", "table"),
        P("replica", None, None),
        P("replica", "table", None),
        P("replica", "table", None),
        P(),
        P(),
        P(),
    )
    out_specs = (P("replica", "table"), P("replica", "table"))
    return jax.shard_map(routed, mesh=mesh, in_specs=in_specs, out_specs=out_specs, check_vma=False)
```

```python
import functools

import jax
import jax.numpy as jnp
from jax import lax
from jax.experimental import pallas as pl
from jax.experimental.pallas import tpu as pltpu
from jax.sharding import PartitionSpec as P

MESH = pl.DeviceIdType.MESH
MXU = 256
LANES = 128
VMEM_BYTES = 64 << 20
F32 = jnp.float32
BF16 = jnp.bfloat16

TILE = 8


EPSILON = 1e-05


def layer_norm(features):
    centre = jnp.mean(features, axis=-1, keepdims=True)
    centred = features - centre
    spread = jnp.mean(centred * centred, axis=-1, keepdims=True)
    return centred * lax.rsqrt(spread + EPSILON)


def segment_ids(lengths, row_count, tile_rows):
    boundary = jnp.cumsum(lengths)
    tile_index = jnp.arange(row_count, dtype=jnp.int32) // tile_rows
    return jnp.sum((tile_index[None, :] >= boundary[:, None]).astype(jnp.int32), axis=0)


def hstu_layer(inputs, segment, slopes, uvqk_weight, out_weight):
    row_count, feature_count = inputs.shape
    head_count = slopes.shape[0]
    head_size = feature_count // head_count
    score_scale = head_size ** (-0.5)
    normed = layer_norm(inputs.astype(jnp.float32)).astype(jnp.bfloat16)
    projected = jax.nn.silu(jnp.dot(normed, uvqk_weight, preferred_element_type=jnp.float32))
    gate_part = projected[:, :feature_count]
    value_part = projected[:, feature_count : 2 * feature_count].astype(jnp.bfloat16)
    query_part = projected[:, 2 * feature_count : 3 * feature_count].astype(jnp.bfloat16)
    key_part = projected[:, 3 * feature_count :].astype(jnp.bfloat16)
    row_index = lax.broadcasted_iota(jnp.int32, (row_count, row_count), 0)
    col_index = lax.broadcasted_iota(jnp.int32, (row_count, row_count), 1)
    allowed = (segment[:, None] == segment[None, :]) & (col_index <= row_index)
    distance = (row_index - col_index).astype(jnp.float32)
    pieces = []
    for head_index in range(head_count):
        lower = head_index * head_size
        upper = lower + head_size
        scores = jnp.dot(
            query_part[:, lower:upper],
            key_part[:, lower:upper].T,
            preferred_element_type=jnp.float32,
        )
        scores = scores * score_scale - slopes[head_index] * distance
        weights = jnp.where(allowed, jax.nn.silu(scores), jnp.zeros_like(scores)).astype(
            jnp.bfloat16
        )
        pieces.append(
            jnp.dot(weights, value_part[:, lower:upper], preferred_element_type=jnp.float32)
        )
    attended = jnp.concatenate(pieces, axis=1)
    gated = (layer_norm(attended) * gate_part).astype(jnp.bfloat16)
    mixing = jnp.dot(gated, out_weight, preferred_element_type=jnp.float32)
    return (inputs.astype(jnp.float32) + mixing).astype(jnp.bfloat16)


def forward_backward(inputs, grad_rows, segment, slopes, uvqk_weight, out_weight):

    def apply_layer(layer_input):
        return hstu_layer(layer_input, segment, slopes, uvqk_weight, out_weight)

    outputs, pullback = jax.vjp(apply_layer, inputs)
    return (outputs, pullback(grad_rows)[0])


def shards(
    embeds, cotangent, send_plan, work_plan, sequence_tiles, slopes, uvqk_weight, out_weight
):
    table_count = lax.axis_size("table")
    replica_count = lax.axis_size("replica")
    column_count = embeds.shape[1]
    row_count = embeds.shape[0] // table_count
    tile_count = row_count // TILE
    peer_rows = row_count // replica_count
    feature_count = column_count * table_count
    block_plans = send_plan[0]
    own_send = lax.dynamic_index_in_dim(block_plans, lax.axis_index("table"), 0, keepdims=False)
    own_work = work_plan[0, 0]
    segment = segment_ids(sequence_tiles[0, 0], row_count, TILE)
    tile_order = jnp.arange(tile_count, dtype=jnp.int32)
    row_inputs, row_grads = (
        lax.all_to_all(embeds, "table", split_axis=0, concat_axis=1, tiled=True),
        lax.all_to_all(cotangent, "table", split_axis=0, concat_axis=1, tiled=True),
    )

    def to_slots(shard_rows):
        tiled = shard_rows.reshape(tile_count, TILE, feature_count)
        return tiled[own_send]

    got_inputs, got_grads = (
        lax.all_to_all(to_slots(row_inputs), "replica", split_axis=0, concat_axis=0, tiled=True),
        lax.all_to_all(to_slots(row_grads), "replica", split_axis=0, concat_axis=0, tiled=True),
    )
    work_inputs = got_inputs[own_work].reshape(row_count, feature_count)
    work_grads = got_grads[own_work].reshape(row_count, feature_count)
    outputs, gradient = forward_backward(
        work_inputs, work_grads, segment, slopes, uvqk_weight, out_weight
    )
    undo_work = jnp.zeros((tile_count,), jnp.int32).at[own_work].set(tile_order)

    def to_sources(result):
        return result.reshape(tile_count, TILE, feature_count)[undo_work]

    slot_outputs = to_sources(outputs)
    slot_grads = to_sources(gradient)
    back_outputs, back_grads = (
        lax.all_to_all(slot_outputs, "replica", split_axis=0, concat_axis=0, tiled=True),
        lax.all_to_all(slot_grads, "replica", split_axis=0, concat_axis=0, tiled=True),
    )
    undo_send = jnp.zeros((tile_count,), jnp.int32).at[own_send].set(tile_order)

    def to_home(result):
        return result[undo_send].reshape(row_count, feature_count)

    layer_output, input_gradient = (
        lax.all_to_all(to_home(back_outputs), "table", split_axis=1, concat_axis=0, tiled=True),
        lax.all_to_all(to_home(back_grads), "table", split_axis=1, concat_axis=0, tiled=True),
    )
    return (layer_output, input_gradient)


NT = (((1,), (1,)), ((), ()))
TN = (((0,), (0,)), ((), ()))


def mm(a, b, dims=(((1,), (0,)), ((), ()))):
    return lax.dot_general(a, b, dims, preferred_element_type=F32)


def norm_parts(features):
    centred = features - jnp.mean(features, axis=-1, keepdims=True)
    scale = lax.rsqrt(jnp.mean(centred * centred, axis=-1, keepdims=True) + EPSILON)
    return centred * scale, scale


def norm_back(grad, normal, scale):
    along = jnp.mean(grad * normal, axis=-1, keepdims=True)
    return scale * (grad - jnp.mean(grad, axis=-1, keepdims=True) - normal * along)


def silu_parts(v):
    sig = 0.5 * jnp.tanh(0.5 * v) + 0.5
    value = v * sig
    return value, sig + value * (1.0 - sig)


def fused_kernel(
    T, R, H,
    send_hbm, work_hbm, seq_hbm, slope_hbm, emb_hbm, cot_hbm, wu_hbm, wo_hbm,
    ret,
    send_ref, work_ref, seq_ref, slope_ref, emb_ref, cot_ref,
    wu, wo, emb_stage, cot_stage, emb_got, cot_got, x_s, dy_s, slope_s,
    out_back, grad_back,
    in_sem, own_sem, send_sem, recv_sem,
):
    n = T * R
    rows = R * TILE
    width = emb_ref.shape[2]
    feat = T * width
    hs = feat // H
    G = max(1, min(H, MXU // max(hs, rows)))
    gw, gr = G * hs, G * rows
    scale = hs ** (-0.5)
    me_t = lax.axis_index("table")
    me_r = lax.axis_index("replica")
    me = me_r * T + me_t

    sources = (send_hbm, emb_hbm, cot_hbm, work_hbm, seq_hbm, slope_hbm, wu_hbm, wo_hbm)
    targets = (send_ref, emb_ref, cot_ref, work_ref, seq_ref, slope_ref, wu, wo)
    loads = [
        pltpu.make_async_copy(source, target, in_sem.at[i])
        for i, (source, target) in enumerate(zip(sources, targets))
    ]
    for load in loads[:6]:
        load.start()

    def partner(own, step, count):
        other, bit = jnp.int32(0), 1
        while bit < count:
            held = lax.rem(lax.div(own, bit), 2)
            other = other + bit * (1 - held if step & bit else held)
            bit = 2 * bit
        return other

    peers = []
    for far in range(R - 1, -1, -1):
        for near in range(T - 1, -1, -1):
            if far or near:
                t, r = partner(me_t, near, T), partner(me_r, far, R)
                peers.append((r * T + t, {"table": t, "replica": r}))

    barrier = pltpu.get_barrier_semaphore()
    for _, device in peers:
        pl.semaphore_signal(barrier, inc=1, device_id=device, device_id_type=MESH)

    def gather(source, target):
        for d in range(R):
            for t in range(T):
                target[d * T + t] = source[t * R + send_ref[0, t, d]]

    for load in loads[:3]:
        load.wait()
    for load in loads[6:]:
        load.start()
    gather(emb_ref, emb_stage)
    gather(cot_ref, cot_stage)
    pl.semaphore_wait(barrier, n - 1)

    def post(src, dst, index, base=0):
        for other, device in peers:
            pltpu.make_async_remote_copy(
                src_ref=src.at[other],
                dst_ref=dst.at[base + me],
                send_sem=send_sem.at[index],
                recv_sem=recv_sem.at[index],
                device_id=device,
                device_id_type=MESH,
            ).start()

    def settle(ref, sem):
        part = ref.at[pl.ds(0, n - 1)]
        pltpu.make_async_copy(part, part, sem).wait()

    def scatter(source, target):
        for s in range(R):
            for t in range(T):
                target[s * T + t] = source[
                    s * TILE : (s + 1) * TILE, t * width : (t + 1) * width
                ].astype(BF16)

    def unpack(source, target):
        for s in range(R):
            for t in range(T):
                target[s * TILE : (s + 1) * TILE, t * width : (t + 1) * width] = source[
                    s * T + t
                ].astype(F32)

    post(emb_stage, emb_got, 0)
    emb_got[me] = emb_stage[me]
    post(cot_stage, cot_got, 1)
    cot_got[me] = cot_stage[me]

    for load in loads[3:6]:
        load.wait()
    bounds = []
    total = jnp.int32(0)
    for j in range(seq_ref.shape[2]):
        total = total + seq_ref[0, 0, j]
        bounds.append(total)

    def places(index):
        slot = index // TILE
        place = jnp.zeros_like(index)
        for w in range(1, R):
            place = jnp.where(slot == work_ref[0, 0, w], w, place)
        segment = jnp.zeros_like(index)
        for bound in bounds:
            segment = segment + (place >= bound).astype(jnp.int32)
        return place * TILE + index % TILE, segment

    row_pos, row_seg = places(lax.broadcasted_iota(jnp.int32, (rows, 1), 0))
    lane = lax.broadcasted_iota(jnp.int32, (1, gr), 1)
    col_pos, col_seg = places(lane % rows)
    distance = (row_pos - col_pos).astype(F32)
    allowed = (row_seg == col_seg) & (col_pos <= row_pos)
    slope_s[...] = jnp.where(allowed, distance, -1.0)
    same_head = (
        lax.broadcasted_iota(jnp.int32, (gr, gw), 0) // rows
        == lax.broadcasted_iota(jnp.int32, (gr, gw), 1) // hs
    )
    head_mask = jnp.where(same_head, 1.0, 0.0)
    head_mask16 = head_mask.astype(BF16)

    def spread(block):
        return jnp.concatenate([block] * G, axis=0) * head_mask16

    def collect(full):
        masked = full * head_mask
        total = masked[:rows]
        for h in range(1, G):
            total = total + masked[h * rows : (h + 1) * rows]
        return total

    settle(emb_got, recv_sem.at[0])
    unpack(emb_got, x_s)
    x = x_s[...]
    normal, x_scale = norm_parts(x)
    normed = normal.astype(BF16)
    for load in loads[6:]:
        load.wait()
    projected, slopes_back = [], []
    for c in range(4):
        block = mm(normed, wu[:, c * feat : (c + 1) * feat])
        value, deriv = silu_parts(block)
        projected.append(value if c == 0 else value.astype(BF16))
        slopes_back.append(deriv)
    gate, value, query, key = projected

    settle(cot_got, recv_sem.at[1])
    unpack(cot_got, dy_s)
    dy = dy_s[...]
    dgated = mm(dy.astype(BF16), wo[...], NT).astype(BF16).astype(F32)

    relative = slope_s[...]
    allowed = relative >= 0.0
    weights, derivs, pieces, values, keys, queries = [], [], [], [], [], []
    for g in range(H // G):
        cs = slice(g * gw, (g + 1) * gw)
        kd, vd, q = spread(key[:, cs]), spread(value[:, cs]), query[:, cs]
        slope = jnp.zeros((1, gr), F32)
        for h in range(G):
            slope = jnp.where(lane // rows == h, slope_ref[g * G + h], slope)
        scores = mm(q, kd, NT) * scale - slope * relative
        weight, deriv = silu_parts(scores)
        weight = jnp.where(allowed, weight, 0.0).astype(BF16)
        derivs.append(jnp.where(allowed, deriv * scale, 0.0))
        weights.append(weight)
        pieces.append(mm(weight, vd))
        keys.append(kd)
        values.append(vd)
        queries.append(q)
    attended, att_scale = norm_parts(jnp.concatenate(pieces, axis=1))
    dgate = dgated * attended
    datt = norm_back(dgated * gate, attended, att_scale).astype(BF16)
    gated = (attended * gate).astype(BF16)
    output = x + mm(gated, wo[...])
    scatter(output, out_back)
    dv, dq, dk = [], [], []
    for g in range(H // G):
        da = datt[:, g * gw : (g + 1) * gw]
        dw = mm(da, values[g], NT).astype(BF16).astype(F32)
        ds = (dw * derivs[g]).astype(BF16)
        dv.append(collect(mm(weights[g], da, TN)))
        dq.append(mm(ds, keys[g]))
        dk.append(collect(mm(ds, queries[g], TN)))
    post(out_back, ret, 2)
    out_own = pltpu.make_async_copy(out_back.at[me], ret.at[me], own_sem.at[0])
    out_own.start()
    dprojected = [dgate] + [
        jnp.concatenate(parts, axis=1).astype(BF16).astype(F32) for parts in (dv, dq, dk)
    ]
    dnormed = jnp.zeros_like(x)
    for c in range(4):
        dz = (dprojected[c] * slopes_back[c]).astype(BF16)
        dnormed = dnormed + mm(dz, wu[:, c * feat : (c + 1) * feat], NT)
    dnormed = dnormed.astype(BF16).astype(F32)
    gradient = norm_back(dnormed, normal, x_scale) + dy

    scatter(gradient, grad_back)
    post(grad_back, ret, 3, n)
    grad_own = pltpu.make_async_copy(grad_back.at[me], ret.at[n + me], own_sem.at[1])
    grad_own.start()
    out_own.wait()
    grad_own.wait()
    for index, source in enumerate((emb_stage, cot_stage, out_back, grad_back)):
        settle(source, send_sem.at[index])
    settle(out_back, recv_sem.at[2])
    settle(grad_back, recv_sem.at[3])


def fused_shards(
    embeds, cotangent, send_plan, work_plan, sequence_tiles, slopes, uvqk_weight, out_weight
):
    T, R = lax.axis_size("table"), lax.axis_size("replica")
    n, rows, width = T * R, R * TILE, embeds.shape[1]
    feat, H = T * width, slopes.shape[0]
    G = max(1, min(H, MXU // max(feat // H, rows)))
    vmem = pl.BlockSpec(memory_space=pltpu.VMEM)
    smem = pl.BlockSpec(memory_space=pltpu.SMEM)
    hbm = pl.BlockSpec(memory_space=pltpu.HBM)
    message = pltpu.VMEM((n, TILE, width), BF16)
    tiles = jax.ShapeDtypeStruct((n, TILE, width), BF16)
    ret = pl.pallas_call(
        functools.partial(fused_kernel, T, R, H),
        out_shape=jax.ShapeDtypeStruct((2 * n, TILE, width), BF16),
        in_specs=[hbm] * 8,
        out_specs=hbm,
        scratch_shapes=[
            pltpu.SMEM(send_plan.shape, jnp.int32),
            pltpu.SMEM(work_plan.shape, jnp.int32),
            pltpu.SMEM(sequence_tiles.shape, jnp.int32),
            pltpu.SMEM(slopes.shape, F32),
            message,
            message,
            pltpu.VMEM(uvqk_weight.shape, BF16),
            pltpu.VMEM(out_weight.shape, BF16),
            message,
            message,
            message,
            message,
            pltpu.VMEM((rows, feat), F32),
            pltpu.VMEM((rows, feat), F32),
            pltpu.VMEM((rows, G * rows), F32),
            message,
            message,
            pltpu.SemaphoreType.DMA((8,)),
            pltpu.SemaphoreType.DMA((2,)),
            pltpu.SemaphoreType.DMA((4,)),
            pltpu.SemaphoreType.DMA((4,)),
        ],
        compiler_params=pltpu.CompilerParams(
            collective_id=0, has_side_effects=True, vmem_limit_bytes=VMEM_BYTES
        ),
        name="hstu_fused",
    )(
        send_plan,
        work_plan,
        sequence_tiles,
        slopes,
        embeds.reshape(tiles.shape),
        cotangent.reshape(tiles.shape),
        uvqk_weight,
        out_weight,
    )
    placed = pl.pallas_call(
        functools.partial(place_kernel, T, R),
        out_shape=(tiles, tiles),
        in_specs=[smem, vmem],
        out_specs=(vmem, vmem),
        compiler_params=pltpu.CompilerParams(vmem_limit_bytes=VMEM_BYTES),
        name="place",
    )(send_plan, ret)
    return tuple(part.reshape(embeds.shape) for part in placed)


def place_kernel(T, R, send_ref, ret_ref, out_ref, grad_ref):
    for t in range(T):
        for d in range(R):
            home = t * R + send_ref[0, t, d]
            out_ref[home] = ret_ref[d * T + t]
            grad_ref[home] = ret_ref[T * R + d * T + t]


def fits_fused(embeds, slopes, T, R):
    width = embeds.shape[1]
    heads = slopes.shape[0]
    row_count = embeds.shape[0] // T
    head_size = width * T // heads
    return (
        width % LANES == 0
        and R & (R - 1) == 0
        and T & (T - 1) == 0
        and row_count == R * TILE
        and head_size == row_count
        and heads % max(1, min(heads, MXU // head_size)) == 0
    )


def routed(embeds, cotangent, send_plan, work_plan, sequence_tiles, slopes, *weights):
    T, R = lax.axis_size("table"), lax.axis_size("replica")
    body = fused_shards if fits_fused(embeds, slopes, T, R) else shards
    return body(embeds, cotangent, send_plan, work_plan, sequence_tiles, slopes, *weights)


def solution(mesh):
    in_specs = (
        P("replica", "table"),
        P("replica", "table"),
        P("replica", None, None),
        P("replica", "table", None),
        P("replica", "table", None),
        P(),
        P(),
        P(),
    )
    out_specs = (P("replica", "table"), P("replica", "table"))
    return jax.shard_map(routed, mesh=mesh, in_specs=in_specs, out_specs=out_specs, check_vma=False)
```

```python
import functools

import jax
import jax.numpy as jnp
from jax import lax
from jax.experimental import pallas as pl
from jax.experimental.pallas import tpu as pltpu
from jax.sharding import PartitionSpec as P

MESH = pl.DeviceIdType.MESH
MXU = 256
LANES = 128
VMEM_BYTES = 64 << 20
F32 = jnp.float32
BF16 = jnp.bfloat16

TILE = 8


EPSILON = 1e-05


def layer_norm(features):
    centre = jnp.mean(features, axis=-1, keepdims=True)
    centred = features - centre
    spread = jnp.mean(centred * centred, axis=-1, keepdims=True)
    return centred * lax.rsqrt(spread + EPSILON)


def segment_ids(lengths, row_count, tile_rows):
    boundary = jnp.cumsum(lengths)
    tile_index = jnp.arange(row_count, dtype=jnp.int32) // tile_rows
    return jnp.sum((tile_index[None, :] >= boundary[:, None]).astype(jnp.int32), axis=0)


def hstu_layer(inputs, segment, slopes, uvqk_weight, out_weight):
    row_count, feature_count = inputs.shape
    head_count = slopes.shape[0]
    head_size = feature_count // head_count
    score_scale = head_size ** (-0.5)
    normed = layer_norm(inputs.astype(jnp.float32)).astype(jnp.bfloat16)
    projected = jax.nn.silu(jnp.dot(normed, uvqk_weight, preferred_element_type=jnp.float32))
    gate_part = projected[:, :feature_count]
    value_part = projected[:, feature_count : 2 * feature_count].astype(jnp.bfloat16)
    query_part = projected[:, 2 * feature_count : 3 * feature_count].astype(jnp.bfloat16)
    key_part = projected[:, 3 * feature_count :].astype(jnp.bfloat16)
    row_index = lax.broadcasted_iota(jnp.int32, (row_count, row_count), 0)
    col_index = lax.broadcasted_iota(jnp.int32, (row_count, row_count), 1)
    allowed = (segment[:, None] == segment[None, :]) & (col_index <= row_index)
    distance = (row_index - col_index).astype(jnp.float32)
    pieces = []
    for head_index in range(head_count):
        lower = head_index * head_size
        upper = lower + head_size
        scores = jnp.dot(
            query_part[:, lower:upper],
            key_part[:, lower:upper].T,
            preferred_element_type=jnp.float32,
        )
        scores = scores * score_scale - slopes[head_index] * distance
        weights = jnp.where(allowed, jax.nn.silu(scores), jnp.zeros_like(scores)).astype(
            jnp.bfloat16
        )
        pieces.append(
            jnp.dot(weights, value_part[:, lower:upper], preferred_element_type=jnp.float32)
        )
    attended = jnp.concatenate(pieces, axis=1)
    gated = (layer_norm(attended) * gate_part).astype(jnp.bfloat16)
    mixing = jnp.dot(gated, out_weight, preferred_element_type=jnp.float32)
    return (inputs.astype(jnp.float32) + mixing).astype(jnp.bfloat16)


def forward_backward(inputs, grad_rows, segment, slopes, uvqk_weight, out_weight):

    def apply_layer(layer_input):
        return hstu_layer(layer_input, segment, slopes, uvqk_weight, out_weight)

    outputs, pullback = jax.vjp(apply_layer, inputs)
    return (outputs, pullback(grad_rows)[0])


def shards(
    embeds, cotangent, send_plan, work_plan, sequence_tiles, slopes, uvqk_weight, out_weight
):
    table_count = lax.axis_size("table")
    replica_count = lax.axis_size("replica")
    column_count = embeds.shape[1]
    row_count = embeds.shape[0] // table_count
    tile_count = row_count // TILE
    peer_rows = row_count // replica_count
    feature_count = column_count * table_count
    block_plans = send_plan[0]
    own_send = lax.dynamic_index_in_dim(block_plans, lax.axis_index("table"), 0, keepdims=False)
    own_work = work_plan[0, 0]
    segment = segment_ids(sequence_tiles[0, 0], row_count, TILE)
    tile_order = jnp.arange(tile_count, dtype=jnp.int32)
    row_inputs, row_grads = (
        lax.all_to_all(embeds, "table", split_axis=0, concat_axis=1, tiled=True),
        lax.all_to_all(cotangent, "table", split_axis=0, concat_axis=1, tiled=True),
    )

    def to_slots(shard_rows):
        tiled = shard_rows.reshape(tile_count, TILE, feature_count)
        return tiled[own_send]

    got_inputs, got_grads = (
        lax.all_to_all(to_slots(row_inputs), "replica", split_axis=0, concat_axis=0, tiled=True),
        lax.all_to_all(to_slots(row_grads), "replica", split_axis=0, concat_axis=0, tiled=True),
    )
    work_inputs = got_inputs[own_work].reshape(row_count, feature_count)
    work_grads = got_grads[own_work].reshape(row_count, feature_count)
    outputs, gradient = forward_backward(
        work_inputs, work_grads, segment, slopes, uvqk_weight, out_weight
    )
    undo_work = jnp.zeros((tile_count,), jnp.int32).at[own_work].set(tile_order)

    def to_sources(result):
        return result.reshape(tile_count, TILE, feature_count)[undo_work]

    slot_outputs = to_sources(outputs)
    slot_grads = to_sources(gradient)
    back_outputs, back_grads = (
        lax.all_to_all(slot_outputs, "replica", split_axis=0, concat_axis=0, tiled=True),
        lax.all_to_all(slot_grads, "replica", split_axis=0, concat_axis=0, tiled=True),
    )
    undo_send = jnp.zeros((tile_count,), jnp.int32).at[own_send].set(tile_order)

    def to_home(result):
        return result[undo_send].reshape(row_count, feature_count)

    layer_output, input_gradient = (
        lax.all_to_all(to_home(back_outputs), "table", split_axis=1, concat_axis=0, tiled=True),
        lax.all_to_all(to_home(back_grads), "table", split_axis=1, concat_axis=0, tiled=True),
    )
    return (layer_output, input_gradient)


NT = (((1,), (1,)), ((), ()))
TN = (((0,), (0,)), ((), ()))


def mm(a, b, dims=(((1,), (0,)), ((), ()))):
    return lax.dot_general(a, b, dims, preferred_element_type=F32)


def norm_parts(features):
    centred = features - jnp.mean(features, axis=-1, keepdims=True)
    scale = lax.rsqrt(jnp.mean(centred * centred, axis=-1, keepdims=True) + EPSILON)
    return centred * scale, scale


def norm_back(grad, normal, scale):
    along = jnp.mean(grad * normal, axis=-1, keepdims=True)
    return scale * (grad - jnp.mean(grad, axis=-1, keepdims=True) - normal * along)


def silu_parts(v):
    sig = 0.5 * jnp.tanh(0.5 * v) + 0.5
    value = v * sig
    return value, sig + value * (1.0 - sig)


def fused_kernel(
    T, R, H,
    send_hbm, work_hbm, seq_hbm, slope_hbm, emb_hbm, cot_hbm, wu_hbm, wo_hbm,
    ret,
    send_ref, work_ref, seq_ref, slope_ref, emb_ref, cot_ref,
    wu, wo, emb_stage, cot_stage, emb_got, cot_got, x_s, dy_s, slope_s,
    out_back, grad_back,
    in_sem, own_sem, send_sem, recv_sem,
):
    n = T * R
    rows = R * TILE
    width = emb_ref.shape[2]
    feat = T * width
    hs = feat // H
    G = max(1, min(H, MXU // max(hs, rows)))
    gw, gr = G * hs, G * rows
    scale = hs ** (-0.5)
    me_t = lax.axis_index("table")
    me_r = lax.axis_index("replica")
    me = me_r * T + me_t

    sources = (send_hbm, emb_hbm, cot_hbm, work_hbm, seq_hbm, slope_hbm, wu_hbm, wo_hbm)
    targets = (send_ref, emb_ref, cot_ref, work_ref, seq_ref, slope_ref, wu, wo)
    loads = [
        pltpu.make_async_copy(source, target, in_sem.at[i])
        for i, (source, target) in enumerate(zip(sources, targets))
    ]
    for load in loads[:6]:
        load.start()

    def partner(own, step, count):
        other, bit = jnp.int32(0), 1
        while bit < count:
            held = lax.rem(lax.div(own, bit), 2)
            other = other + bit * (1 - held if step & bit else held)
            bit = 2 * bit
        return other

    peers = []
    for far in range(R - 1, -1, -1):
        for near in range(T - 1, -1, -1):
            if far or near:
                t, r = partner(me_t, near, T), partner(me_r, far, R)
                peers.append((r * T + t, {"table": t, "replica": r}))

    barrier = pltpu.get_barrier_semaphore()
    for _, device in peers:
        pl.semaphore_signal(barrier, inc=1, device_id=device, device_id_type=MESH)

    def gather(source, target):
        for d in range(R):
            for t in range(T):
                target[d * T + t] = source[t * R + send_ref[0, t, d]]

    for load in loads[:3]:
        load.wait()
    for load in loads[6:]:
        load.start()
    gather(emb_ref, emb_stage)
    gather(cot_ref, cot_stage)
    pl.semaphore_wait(barrier, n - 1)

    def post(src, dst, index, base=0):
        for other, device in peers:
            pltpu.make_async_remote_copy(
                src_ref=src.at[other],
                dst_ref=dst.at[base + me],
                send_sem=send_sem.at[index],
                recv_sem=recv_sem.at[index],
                device_id=device,
                device_id_type=MESH,
            ).start()

    def settle(ref, sem):
        part = ref.at[pl.ds(0, n - 1)]
        pltpu.make_async_copy(part, part, sem).wait()

    def scatter(source, target):
        for s in range(R):
            for t in range(T):
                target[s * T + t] = source[
                    s * TILE : (s + 1) * TILE, t * width : (t + 1) * width
                ].astype(BF16)

    def unpack(source, target):
        for s in range(R):
            for t in range(T):
                target[s * TILE : (s + 1) * TILE, t * width : (t + 1) * width] = source[
                    s * T + t
                ].astype(F32)

    post(emb_stage, emb_got, 0)
    emb_got[me] = emb_stage[me]
    post(cot_stage, cot_got, 1)
    cot_got[me] = cot_stage[me]

    for load in loads[3:6]:
        load.wait()
    bounds = []
    total = jnp.int32(0)
    for j in range(seq_ref.shape[2]):
        total = total + seq_ref[0, 0, j]
        bounds.append(total)

    def places(index):
        slot = index // TILE
        place = jnp.zeros_like(index)
        for w in range(1, R):
            place = jnp.where(slot == work_ref[0, 0, w], w, place)
        segment = jnp.zeros_like(index)
        for bound in bounds:
            segment = segment + (place >= bound).astype(jnp.int32)
        return place * TILE + index % TILE, segment

    row_pos, row_seg = places(lax.broadcasted_iota(jnp.int32, (rows, 1), 0))
    lane = lax.broadcasted_iota(jnp.int32, (1, gr), 1)
    col_pos, col_seg = places(lane % rows)
    distance = (row_pos - col_pos).astype(F32)
    allowed = (row_seg == col_seg) & (col_pos <= row_pos)
    slope_s[...] = jnp.where(allowed, distance, -1.0)
    same_head = (
        lax.broadcasted_iota(jnp.int32, (gr, gw), 0) // rows
        == lax.broadcasted_iota(jnp.int32, (gr, gw), 1) // hs
    )
    head_mask = jnp.where(same_head, 1.0, 0.0)
    head_mask16 = head_mask.astype(BF16)

    def spread(block):
        return jnp.concatenate([block] * G, axis=0) * head_mask16

    def collect(full):
        masked = full * head_mask
        total = masked[:rows]
        for h in range(1, G):
            total = total + masked[h * rows : (h + 1) * rows]
        return total

    settle(emb_got, recv_sem.at[0])
    unpack(emb_got, x_s)
    x = x_s[...]
    normal, x_scale = norm_parts(x)
    normed = normal.astype(BF16)
    for load in loads[6:]:
        load.wait()
    projected, slopes_back = [], []
    for c in range(4):
        block = mm(normed, wu[:, c * feat : (c + 1) * feat])
        value, deriv = silu_parts(block)
        projected.append(value if c == 0 else value.astype(BF16))
        slopes_back.append(deriv)
    gate, value, query, key = projected

    relative = slope_s[...]
    allowed = relative >= 0.0
    weights, derivs, pieces, values, keys, queries = [], [], [], [], [], []
    for g in range(H // G):
        cs = slice(g * gw, (g + 1) * gw)
        kd, vd, q = spread(key[:, cs]), spread(value[:, cs]), query[:, cs]
        slope = jnp.zeros((1, gr), F32)
        for h in range(G):
            slope = jnp.where(lane // rows == h, slope_ref[g * G + h], slope)
        scores = mm(q, kd, NT) * scale - slope * relative
        weight, deriv = silu_parts(scores)
        weight = jnp.where(allowed, weight, 0.0).astype(BF16)
        derivs.append(jnp.where(allowed, deriv * scale, 0.0))
        weights.append(weight)
        pieces.append(mm(weight, vd))
        keys.append(kd)
        values.append(vd)
        queries.append(q)
    settle(cot_got, recv_sem.at[1])
    unpack(cot_got, dy_s)
    dy = dy_s[...]
    dgated = mm(dy.astype(BF16), wo[...], NT).astype(BF16).astype(F32)
    attended, att_scale = norm_parts(jnp.concatenate(pieces, axis=1))
    dgate = dgated * attended
    datt = norm_back(dgated * gate, attended, att_scale).astype(BF16)
    gated = (attended * gate).astype(BF16)
    output = x + mm(gated, wo[...])
    scatter(output, out_back)
    dv, dq, dk = [], [], []
    for g in range(H // G):
        da = datt[:, g * gw : (g + 1) * gw]
        dw = mm(da, values[g], NT).astype(BF16).astype(F32)
        ds = (dw * derivs[g]).astype(BF16)
        dv.append(collect(mm(weights[g], da, TN)))
        dq.append(mm(ds, keys[g]))
        dk.append(collect(mm(ds, queries[g], TN)))
    post(out_back, ret, 2)
    out_own = pltpu.make_async_copy(out_back.at[me], ret.at[me], own_sem.at[0])
    out_own.start()
    dprojected = [dgate] + [
        jnp.concatenate(parts, axis=1).astype(BF16).astype(F32) for parts in (dv, dq, dk)
    ]
    dnormed = jnp.zeros_like(x)
    for c in range(4):
        dz = (dprojected[c] * slopes_back[c]).astype(BF16)
        dnormed = dnormed + mm(dz, wu[:, c * feat : (c + 1) * feat], NT)
    dnormed = dnormed.astype(BF16).astype(F32)
    gradient = norm_back(dnormed, normal, x_scale) + dy

    scatter(gradient, grad_back)
    post(grad_back, ret, 3, n)
    grad_own = pltpu.make_async_copy(grad_back.at[me], ret.at[n + me], own_sem.at[1])
    grad_own.start()
    out_own.wait()
    grad_own.wait()
    for index, source in enumerate((emb_stage, cot_stage, out_back, grad_back)):
        settle(source, send_sem.at[index])
    settle(out_back, recv_sem.at[2])
    settle(grad_back, recv_sem.at[3])


def fused_shards(
    embeds, cotangent, send_plan, work_plan, sequence_tiles, slopes, uvqk_weight, out_weight
):
    T, R = lax.axis_size("table"), lax.axis_size("replica")
    n, rows, width = T * R, R * TILE, embeds.shape[1]
    feat, H = T * width, slopes.shape[0]
    G = max(1, min(H, MXU // max(feat // H, rows)))
    vmem = pl.BlockSpec(memory_space=pltpu.VMEM)
    smem = pl.BlockSpec(memory_space=pltpu.SMEM)
    hbm = pl.BlockSpec(memory_space=pltpu.HBM)
    message = pltpu.VMEM((n, TILE, width), BF16)
    tiles = jax.ShapeDtypeStruct((n, TILE, width), BF16)
    ret = pl.pallas_call(
        functools.partial(fused_kernel, T, R, H),
        out_shape=jax.ShapeDtypeStruct((2 * n, TILE, width), BF16),
        in_specs=[hbm] * 8,
        out_specs=hbm,
        scratch_shapes=[
            pltpu.SMEM(send_plan.shape, jnp.int32),
            pltpu.SMEM(work_plan.shape, jnp.int32),
            pltpu.SMEM(sequence_tiles.shape, jnp.int32),
            pltpu.SMEM(slopes.shape, F32),
            message,
            message,
            pltpu.VMEM(uvqk_weight.shape, BF16),
            pltpu.VMEM(out_weight.shape, BF16),
            message,
            message,
            message,
            message,
            pltpu.VMEM((rows, feat), F32),
            pltpu.VMEM((rows, feat), F32),
            pltpu.VMEM((rows, G * rows), F32),
            message,
            message,
            pltpu.SemaphoreType.DMA((8,)),
            pltpu.SemaphoreType.DMA((2,)),
            pltpu.SemaphoreType.DMA((4,)),
            pltpu.SemaphoreType.DMA((4,)),
        ],
        compiler_params=pltpu.CompilerParams(
            collective_id=0, has_side_effects=True, vmem_limit_bytes=VMEM_BYTES
        ),
        name="hstu_fused",
    )(
        send_plan,
        work_plan,
        sequence_tiles,
        slopes,
        embeds.reshape(tiles.shape),
        cotangent.reshape(tiles.shape),
        uvqk_weight,
        out_weight,
    )
    placed = pl.pallas_call(
        functools.partial(place_kernel, T, R),
        out_shape=(tiles, tiles),
        in_specs=[smem, vmem],
        out_specs=(vmem, vmem),
        compiler_params=pltpu.CompilerParams(vmem_limit_bytes=VMEM_BYTES),
        name="place",
    )(send_plan, ret)
    return tuple(part.reshape(embeds.shape) for part in placed)


def place_kernel(T, R, send_ref, ret_ref, out_ref, grad_ref):
    for t in range(T):
        for d in range(R):
            home = t * R + send_ref[0, t, d]
            out_ref[home] = ret_ref[d * T + t]
            grad_ref[home] = ret_ref[T * R + d * T + t]


def fits_fused(embeds, slopes, T, R):
    width = embeds.shape[1]
    heads = slopes.shape[0]
    row_count = embeds.shape[0] // T
    head_size = width * T // heads
    return (
        width % LANES == 0
        and R & (R - 1) == 0
        and T & (T - 1) == 0
        and row_count == R * TILE
        and head_size == row_count
        and heads % max(1, min(heads, MXU // head_size)) == 0
    )


def routed(embeds, cotangent, send_plan, work_plan, sequence_tiles, slopes, *weights):
    T, R = lax.axis_size("table"), lax.axis_size("replica")
    body = fused_shards if fits_fused(embeds, slopes, T, R) else shards
    return body(embeds, cotangent, send_plan, work_plan, sequence_tiles, slopes, *weights)


def solution(mesh):
    in_specs = (
        P("replica", "table"),
        P("replica", "table"),
        P("replica", None, None),
        P("replica", "table", None),
        P("replica", "table", None),
        P(),
        P(),
        P(),
    )
    out_specs = (P("replica", "table"), P("replica", "table"))
    return jax.shard_map(routed, mesh=mesh, in_specs=in_specs, out_specs=out_specs, check_vma=False)
```

```python
import functools

import jax
import jax.numpy as jnp
from jax import lax
from jax.experimental import pallas as pl
from jax.experimental.pallas import tpu as pltpu
from jax.sharding import PartitionSpec as P

MESH = pl.DeviceIdType.MESH
MXU = 256
LANES = 128
VMEM_BYTES = 64 << 20
F32 = jnp.float32
BF16 = jnp.bfloat16

TILE = 8


EPSILON = 1e-05


def layer_norm(features):
    centre = jnp.mean(features, axis=-1, keepdims=True)
    centred = features - centre
    spread = jnp.mean(centred * centred, axis=-1, keepdims=True)
    return centred * lax.rsqrt(spread + EPSILON)


def segment_ids(lengths, row_count, tile_rows):
    boundary = jnp.cumsum(lengths)
    tile_index = jnp.arange(row_count, dtype=jnp.int32) // tile_rows
    return jnp.sum((tile_index[None, :] >= boundary[:, None]).astype(jnp.int32), axis=0)


def hstu_layer(inputs, segment, slopes, uvqk_weight, out_weight):
    row_count, feature_count = inputs.shape
    head_count = slopes.shape[0]
    head_size = feature_count // head_count
    score_scale = head_size ** (-0.5)
    normed = layer_norm(inputs.astype(jnp.float32)).astype(jnp.bfloat16)
    projected = jax.nn.silu(jnp.dot(normed, uvqk_weight, preferred_element_type=jnp.float32))
    gate_part = projected[:, :feature_count]
    value_part = projected[:, feature_count : 2 * feature_count].astype(jnp.bfloat16)
    query_part = projected[:, 2 * feature_count : 3 * feature_count].astype(jnp.bfloat16)
    key_part = projected[:, 3 * feature_count :].astype(jnp.bfloat16)
    row_index = lax.broadcasted_iota(jnp.int32, (row_count, row_count), 0)
    col_index = lax.broadcasted_iota(jnp.int32, (row_count, row_count), 1)
    allowed = (segment[:, None] == segment[None, :]) & (col_index <= row_index)
    distance = (row_index - col_index).astype(jnp.float32)
    pieces = []
    for head_index in range(head_count):
        lower = head_index * head_size
        upper = lower + head_size
        scores = jnp.dot(
            query_part[:, lower:upper],
            key_part[:, lower:upper].T,
            preferred_element_type=jnp.float32,
        )
        scores = scores * score_scale - slopes[head_index] * distance
        weights = jnp.where(allowed, jax.nn.silu(scores), jnp.zeros_like(scores)).astype(
            jnp.bfloat16
        )
        pieces.append(
            jnp.dot(weights, value_part[:, lower:upper], preferred_element_type=jnp.float32)
        )
    attended = jnp.concatenate(pieces, axis=1)
    gated = (layer_norm(attended) * gate_part).astype(jnp.bfloat16)
    mixing = jnp.dot(gated, out_weight, preferred_element_type=jnp.float32)
    return (inputs.astype(jnp.float32) + mixing).astype(jnp.bfloat16)


def forward_backward(inputs, grad_rows, segment, slopes, uvqk_weight, out_weight):

    def apply_layer(layer_input):
        return hstu_layer(layer_input, segment, slopes, uvqk_weight, out_weight)

    outputs, pullback = jax.vjp(apply_layer, inputs)
    return (outputs, pullback(grad_rows)[0])


def shards(
    embeds, cotangent, send_plan, work_plan, sequence_tiles, slopes, uvqk_weight, out_weight
):
    table_count = lax.axis_size("table")
    replica_count = lax.axis_size("replica")
    column_count = embeds.shape[1]
    row_count = embeds.shape[0] // table_count
    tile_count = row_count // TILE
    peer_rows = row_count // replica_count
    feature_count = column_count * table_count
    block_plans = send_plan[0]
    own_send = lax.dynamic_index_in_dim(block_plans, lax.axis_index("table"), 0, keepdims=False)
    own_work = work_plan[0, 0]
    segment = segment_ids(sequence_tiles[0, 0], row_count, TILE)
    tile_order = jnp.arange(tile_count, dtype=jnp.int32)
    row_inputs, row_grads = (
        lax.all_to_all(embeds, "table", split_axis=0, concat_axis=1, tiled=True),
        lax.all_to_all(cotangent, "table", split_axis=0, concat_axis=1, tiled=True),
    )

    def to_slots(shard_rows):
        tiled = shard_rows.reshape(tile_count, TILE, feature_count)
        return tiled[own_send]

    got_inputs, got_grads = (
        lax.all_to_all(to_slots(row_inputs), "replica", split_axis=0, concat_axis=0, tiled=True),
        lax.all_to_all(to_slots(row_grads), "replica", split_axis=0, concat_axis=0, tiled=True),
    )
    work_inputs = got_inputs[own_work].reshape(row_count, feature_count)
    work_grads = got_grads[own_work].reshape(row_count, feature_count)
    outputs, gradient = forward_backward(
        work_inputs, work_grads, segment, slopes, uvqk_weight, out_weight
    )
    undo_work = jnp.zeros((tile_count,), jnp.int32).at[own_work].set(tile_order)

    def to_sources(result):
        return result.reshape(tile_count, TILE, feature_count)[undo_work]

    slot_outputs = to_sources(outputs)
    slot_grads = to_sources(gradient)
    back_outputs, back_grads = (
        lax.all_to_all(slot_outputs, "replica", split_axis=0, concat_axis=0, tiled=True),
        lax.all_to_all(slot_grads, "replica", split_axis=0, concat_axis=0, tiled=True),
    )
    undo_send = jnp.zeros((tile_count,), jnp.int32).at[own_send].set(tile_order)

    def to_home(result):
        return result[undo_send].reshape(row_count, feature_count)

    layer_output, input_gradient = (
        lax.all_to_all(to_home(back_outputs), "table", split_axis=1, concat_axis=0, tiled=True),
        lax.all_to_all(to_home(back_grads), "table", split_axis=1, concat_axis=0, tiled=True),
    )
    return (layer_output, input_gradient)


NT = (((1,), (1,)), ((), ()))
TN = (((0,), (0,)), ((), ()))


def mm(a, b, dims=(((1,), (0,)), ((), ()))):
    return lax.dot_general(a, b, dims, preferred_element_type=F32)


def norm_parts(features):
    centred = features - jnp.mean(features, axis=-1, keepdims=True)
    scale = lax.rsqrt(jnp.mean(centred * centred, axis=-1, keepdims=True) + EPSILON)
    return centred * scale, scale


def norm_back(grad, normal, scale):
    along = jnp.mean(grad * normal, axis=-1, keepdims=True)
    return scale * (grad - jnp.mean(grad, axis=-1, keepdims=True) - normal * along)


def silu_parts(v):
    sig = 0.5 * jnp.tanh(0.5 * v) + 0.5
    value = v * sig
    return value, sig + value * (1.0 - sig)


def fused_kernel(
    T, R, H,
    send_hbm, work_hbm, seq_hbm, slope_hbm, emb_hbm, cot_hbm, wu_hbm, wo_hbm,
    ret,
    send_ref, work_ref, seq_ref, slope_ref, emb_ref, cot_ref,
    wu, wo, emb_stage, cot_stage, emb_got, cot_got, x_s, dy_s, slope_s,
    out_back, grad_back,
    in_sem, own_sem, send_sem, recv_sem,
):
    n = T * R
    rows = R * TILE
    width = emb_ref.shape[2]
    feat = T * width
    hs = feat // H
    G = max(1, min(H, MXU // max(hs, rows)))
    gw, gr = G * hs, G * rows
    scale = hs ** (-0.5)
    me_t = lax.axis_index("table")
    me_r = lax.axis_index("replica")
    me = me_r * T + me_t

    sources = (send_hbm, emb_hbm, cot_hbm, work_hbm, seq_hbm, slope_hbm, wu_hbm, wo_hbm)
    targets = (send_ref, emb_ref, cot_ref, work_ref, seq_ref, slope_ref, wu, wo)
    loads = [
        pltpu.make_async_copy(source, target, in_sem.at[i])
        for i, (source, target) in enumerate(zip(sources, targets))
    ]
    for load in loads[:6]:
        load.start()

    def partner(own, step, count):
        other, bit = jnp.int32(0), 1
        while bit < count:
            held = lax.rem(lax.div(own, bit), 2)
            other = other + bit * (1 - held if step & bit else held)
            bit = 2 * bit
        return other

    peers = []
    for far in range(R - 1, -1, -1):
        for near in range(T - 1, -1, -1):
            if far or near:
                t, r = partner(me_t, near, T), partner(me_r, far, R)
                peers.append((r * T + t, {"table": t, "replica": r}))

    barrier = pltpu.get_barrier_semaphore()
    for _, device in peers:
        pl.semaphore_signal(barrier, inc=1, device_id=device, device_id_type=MESH)

    def gather(source, target):
        for d in range(R):
            for t in range(T):
                target[d * T + t] = source[t * R + send_ref[0, t, d]]

    for load in loads[:3]:
        load.wait()
    for load in loads[6:]:
        load.start()
    gather(emb_ref, emb_stage)
    gather(cot_ref, cot_stage)
    pl.semaphore_wait(barrier, n - 1)

    def post(src, dst, index, base=0):
        for other, device in peers:
            pltpu.make_async_remote_copy(
                src_ref=src.at[other],
                dst_ref=dst.at[base + me],
                send_sem=send_sem.at[index],
                recv_sem=recv_sem.at[index],
                device_id=device,
                device_id_type=MESH,
            ).start()

    def settle(ref, sem):
        part = ref.at[pl.ds(0, n - 1)]
        pltpu.make_async_copy(part, part, sem).wait()

    def scatter(source, target):
        for s in range(R):
            for t in range(T):
                target[s * T + t] = source[
                    s * TILE : (s + 1) * TILE, t * width : (t + 1) * width
                ].astype(BF16)

    def unpack(source, target):
        for s in range(R):
            for t in range(T):
                target[s * TILE : (s + 1) * TILE, t * width : (t + 1) * width] = source[
                    s * T + t
                ].astype(F32)

    post(emb_stage, emb_got, 0)
    emb_got[me] = emb_stage[me]
    post(cot_stage, cot_got, 1)
    cot_got[me] = cot_stage[me]

    for load in loads[3:6]:
        load.wait()
    bounds = []
    total = jnp.int32(0)
    for j in range(seq_ref.shape[2]):
        total = total + seq_ref[0, 0, j]
        bounds.append(total)

    def places(index):
        slot = index // TILE
        place = jnp.zeros_like(index)
        for w in range(1, R):
            place = jnp.where(slot == work_ref[0, 0, w], w, place)
        segment = jnp.zeros_like(index)
        for bound in bounds:
            segment = segment + (place >= bound).astype(jnp.int32)
        return place * TILE + index % TILE, segment

    row_pos, row_seg = places(lax.broadcasted_iota(jnp.int32, (rows, 1), 0))
    lane = lax.broadcasted_iota(jnp.int32, (1, gr), 1)
    col_pos, col_seg = places(lane % rows)
    distance = (row_pos - col_pos).astype(F32)
    allowed = (row_seg == col_seg) & (col_pos <= row_pos)
    slope_s[...] = jnp.where(allowed, distance, -1.0)
    same_head = (
        lax.broadcasted_iota(jnp.int32, (gr, gw), 0) // rows
        == lax.broadcasted_iota(jnp.int32, (gr, gw), 1) // hs
    )
    head_mask = jnp.where(same_head, 1.0, 0.0)
    head_mask16 = head_mask.astype(BF16)

    def spread(block):
        return jnp.concatenate([block] * G, axis=0) * head_mask16

    def collect(full):
        masked = full * head_mask
        total = masked[:rows]
        for h in range(1, G):
            total = total + masked[h * rows : (h + 1) * rows]
        return total

    settle(emb_got, recv_sem.at[0])
    unpack(emb_got, x_s)
    x = x_s[...]
    normal, x_scale = norm_parts(x)
    normed = normal.astype(BF16)
    for load in loads[6:]:
        load.wait()
    projected, slopes_back = [], []
    for c in range(4):
        block = mm(normed, wu[:, c * feat : (c + 1) * feat])
        value, deriv = silu_parts(block)
        projected.append(value if c == 0 else value.astype(BF16))
        slopes_back.append(deriv)
    gate, value, query, key = projected

    relative = slope_s[...]
    allowed = relative >= 0.0
    weights, derivs, pieces, values, keys, queries = [], [], [], [], [], []
    for g in range(H // G):
        cs = slice(g * gw, (g + 1) * gw)
        kd, vd, q = spread(key[:, cs]), spread(value[:, cs]), query[:, cs]
        slope = jnp.zeros((1, gr), F32)
        for h in range(G):
            slope = jnp.where(lane // rows == h, slope_ref[g * G + h], slope)
        scores = mm(q, kd, NT) * scale - slope * relative
        weight, deriv = silu_parts(scores)
        weight = jnp.where(allowed, weight, 0.0).astype(BF16)
        derivs.append(jnp.where(allowed, deriv * scale, 0.0))
        weights.append(weight)
        pieces.append(mm(weight, vd))
        keys.append(kd)
        values.append(vd)
        queries.append(q)
    settle(cot_got, recv_sem.at[1])
    unpack(cot_got, dy_s)
    dy = dy_s[...]
    dgated = mm(dy.astype(BF16), wo[...], NT).astype(BF16).astype(F32)
    attended, att_scale = norm_parts(jnp.concatenate(pieces, axis=1))
    dgate = dgated * attended
    datt = norm_back(dgated * gate, attended, att_scale).astype(BF16)
    gated = (attended * gate).astype(BF16)
    output = x + mm(gated, wo[...])
    scatter(output, out_back)
    post(out_back, ret, 2)
    out_own = pltpu.make_async_copy(out_back.at[me], ret.at[me], own_sem.at[0])
    out_own.start()
    dv, dq, dk = [], [], []
    for g in range(H // G):
        da = datt[:, g * gw : (g + 1) * gw]
        dw = mm(da, values[g], NT).astype(BF16).astype(F32)
        ds = (dw * derivs[g]).astype(BF16)
        dv.append(collect(mm(weights[g], da, TN)))
        dq.append(mm(ds, keys[g]))
        dk.append(collect(mm(ds, queries[g], TN)))
    dprojected = [dgate] + [
        jnp.concatenate(parts, axis=1).astype(BF16).astype(F32) for parts in (dv, dq, dk)
    ]
    dnormed = jnp.zeros_like(x)
    for c in range(4):
        dz = (dprojected[c] * slopes_back[c]).astype(BF16)
        dnormed = dnormed + mm(dz, wu[:, c * feat : (c + 1) * feat], NT)
    dnormed = dnormed.astype(BF16).astype(F32)
    gradient = norm_back(dnormed, normal, x_scale) + dy

    scatter(gradient, grad_back)
    post(grad_back, ret, 3, n)
    grad_own = pltpu.make_async_copy(grad_back.at[me], ret.at[n + me], own_sem.at[1])
    grad_own.start()
    out_own.wait()
    grad_own.wait()
    for index, source in enumerate((emb_stage, cot_stage, out_back, grad_back)):
        settle(source, send_sem.at[index])
    settle(out_back, recv_sem.at[2])
    settle(grad_back, recv_sem.at[3])


def fused_shards(
    embeds, cotangent, send_plan, work_plan, sequence_tiles, slopes, uvqk_weight, out_weight
):
    T, R = lax.axis_size("table"), lax.axis_size("replica")
    n, rows, width = T * R, R * TILE, embeds.shape[1]
    feat, H = T * width, slopes.shape[0]
    G = max(1, min(H, MXU // max(feat // H, rows)))
    vmem = pl.BlockSpec(memory_space=pltpu.VMEM)
    smem = pl.BlockSpec(memory_space=pltpu.SMEM)
    hbm = pl.BlockSpec(memory_space=pltpu.HBM)
    message = pltpu.VMEM((n, TILE, width), BF16)
    tiles = jax.ShapeDtypeStruct((n, TILE, width), BF16)
    ret = pl.pallas_call(
        functools.partial(fused_kernel, T, R, H),
        out_shape=jax.ShapeDtypeStruct((2 * n, TILE, width), BF16),
        in_specs=[hbm] * 8,
        out_specs=hbm,
        scratch_shapes=[
            pltpu.SMEM(send_plan.shape, jnp.int32),
            pltpu.SMEM(work_plan.shape, jnp.int32),
            pltpu.SMEM(sequence_tiles.shape, jnp.int32),
            pltpu.SMEM(slopes.shape, F32),
            message,
            message,
            pltpu.VMEM(uvqk_weight.shape, BF16),
            pltpu.VMEM(out_weight.shape, BF16),
            message,
            message,
            message,
            message,
            pltpu.VMEM((rows, feat), F32),
            pltpu.VMEM((rows, feat), F32),
            pltpu.VMEM((rows, G * rows), F32),
            message,
            message,
            pltpu.SemaphoreType.DMA((8,)),
            pltpu.SemaphoreType.DMA((2,)),
            pltpu.SemaphoreType.DMA((4,)),
            pltpu.SemaphoreType.DMA((4,)),
        ],
        compiler_params=pltpu.CompilerParams(
            collective_id=0, has_side_effects=True, vmem_limit_bytes=VMEM_BYTES
        ),
        name="hstu_fused",
    )(
        send_plan,
        work_plan,
        sequence_tiles,
        slopes,
        embeds.reshape(tiles.shape),
        cotangent.reshape(tiles.shape),
        uvqk_weight,
        out_weight,
    )
    placed = pl.pallas_call(
        functools.partial(place_kernel, T, R),
        out_shape=(tiles, tiles),
        in_specs=[smem, vmem],
        out_specs=(vmem, vmem),
        compiler_params=pltpu.CompilerParams(vmem_limit_bytes=VMEM_BYTES),
        name="place",
    )(send_plan, ret)
    return tuple(part.reshape(embeds.shape) for part in placed)


def place_kernel(T, R, send_ref, ret_ref, out_ref, grad_ref):
    for t in range(T):
        for d in range(R):
            home = t * R + send_ref[0, t, d]
            out_ref[home] = ret_ref[d * T + t]
            grad_ref[home] = ret_ref[T * R + d * T + t]


def fits_fused(embeds, slopes, T, R):
    width = embeds.shape[1]
    heads = slopes.shape[0]
    row_count = embeds.shape[0] // T
    head_size = width * T // heads
    return (
        width % LANES == 0
        and R & (R - 1) == 0
        and T & (T - 1) == 0
        and row_count == R * TILE
        and head_size == row_count
        and heads % max(1, min(heads, MXU // head_size)) == 0
    )


def routed(embeds, cotangent, send_plan, work_plan, sequence_tiles, slopes, *weights):
    T, R = lax.axis_size("table"), lax.axis_size("replica")
    body = fused_shards if fits_fused(embeds, slopes, T, R) else shards
    return body(embeds, cotangent, send_plan, work_plan, sequence_tiles, slopes, *weights)


def solution(mesh):
    in_specs = (
        P("replica", "table"),
        P("replica", "table"),
        P("replica", None, None),
        P("replica", "table", None),
        P("replica", "table", None),
        P(),
        P(),
        P(),
    )
    out_specs = (P("replica", "table"), P("replica", "table"))
    return jax.shard_map(routed, mesh=mesh, in_specs=in_specs, out_specs=out_specs, check_vma=False)
```
